32 devices in a mesh: gx: 8 (over z, y), gy: 4 (over x, core).
Axes of the slice: x: 2, y: 2, z: 4, core: 2. Of those that a mesh axis runs over, the one named last changes fastest.
Arguments:
- fields: float32 [5, 64, 128, 512], P(None, None, 'gx', 'gy'), may hold values from -6 to 6
- previous: float32 [5, 64, 128, 512], P(None, None, 'gx', 'gy'), may hold values from -6 to 6
- heights: int32 [128, 512], P('gx', 'gy'), may hold values from 0 to 32, as said below
- part_cells: int32 [8, 4, 9216], P('gx', 'gy'), may hold values from 0 to 131071, as said below
- part_offsets: float32 [3, 8, 4, 9216], P(None, 'gx', 'gy'), may hold values from 0 to 1
- cross_counts: int32 [8, 4, 2], P('gx', 'gy'), may hold values from 0 to 512, as said below
Outputs:
- updated: float32 [5, 64, 128, 512], P(None, None, 'gx', 'gy')
- accumulated: float32 [5, 64, 128, 512], P(None, None, 'gx', 'gy')
- part_moved: float32 [3, 8, 4, 9216], P(None, 'gx', 'gy')
The draws below stay inside these ranges and needn't reach their ends.
Inputs may be any that keep to these rules, and one draw needn't show every extreme that they name: `heights`: 0 for open ground; some column reaches 32. `part_cells`: the slots 8192 to 8703 lie in the last along-wind cell plane of their device, the slots from 8704 on in the first; slots 8192 and 8704 lie in the last cross-wind column. `cross_counts`: some device has 512 downwind crossers.
All inputs are finite; a program needn't handle non-finite values. Where the reference program divides by a largest or mean magnitude, that divisor is 1e-20 or more.
Results may differ from the reference program's by a relative error of at most 0.00007.
Values sent between devices are 32-bit elements; how exact they have to be, the bound alone decides.
A program may use at most 128 MiB of HBM per device.

```python
import jax
import jax.numpy as jnp
from jax import lax

CX = 16
CY = 128
NZ = 64
P_KEEP = 8192
CAP = 512
P_DEV = 9216
NX = 128
NY = 512
N_GX = 8
N_GY = 4


def draw_heights(key, part):
    key = jax.random.fold_in(key, 1)
    first, second = jax.random.split(key)
    built = jax.random.randint(first, (NX, NY), 0, 5) >= 3
    tall = jax.random.randint(second, (NX, NY), 1, NZ // 2 + 1)
    heights = jnp.where(built, tall, 0).astype(jnp.int32)
    return heights.at[0, 0].set(NZ // 2)


def draw_part_cells(key, part):
    key = jax.random.fold_in(key, 2)
    first, second, third = jax.random.split(key, 3)
    shape = (N_GX, N_GY, P_DEV)
    level_ids = jax.random.randint(first, shape, 0, NZ)
    col_ids = jax.random.randint(second, shape, 0, CY)
    row_ids = jax.random.randint(third, shape, 0, CX)
    slot_index = lax.broadcasted_iota(jnp.int32, shape, 2)
    row_ids = jnp.where(slot_index >= P_KEEP + CAP, 0, jnp.where(slot_index >= P_KEEP, CX - 1, row_ids))
    edge_slot = (slot_index == P_KEEP) | (slot_index == P_KEEP + CAP)
    col_ids = jnp.where(edge_slot, CY - 1, col_ids)
    cells = (level_ids * CX * CY + row_ids * CY + col_ids).astype(jnp.int32)
    cells = cells.at[0, 0, 0].set(NZ * CX * CY - 1)
    return cells.at[0, 0, 1].set(0)


def draw_cross_counts(key, part):
    key = jax.random.fold_in(key, 3)
    counts = jax.random.randint(key, (N_GX, N_GY, 2), 0, CAP + 1).astype(jnp.int32)
    return counts.at[0, 0, 0].set(CAP)


def block_levels(own_key, dims, pieces, least, top_value):
    loudness, own = 1.0, jax.random.fold_in(own_key, 6)
    for position, shards_of in pieces:
        steps = jnp.exp(jax.random.uniform(jax.random.fold_in(own, position), (shards_of,), jnp.float32, least / len(pieces), top_value / len(pieces)))
        loudness = loudness * jnp.repeat(steps, dims[position] // shards_of).reshape([-1 if axis == position else 1 for axis in range(len(dims))])
    return loudness


def centred(own_key, extent, width, most, cuts=(), kind=jnp.bfloat16):
    drawn = width * jax.random.normal(own_key, extent, jnp.float32)
    if cuts:
        drawn = drawn * block_levels(own_key, extent, cuts, -0.22, 0.18)
    return jnp.clip(drawn, -most, most).astype(kind)


def setup_inputs(seed: int = 0) -> dict:
    arg_keys = jax.random.split(jax.random.key(seed), 7)
    return {
        "fields": centred(arg_keys[0], (5, NZ, NX, NY), 1.0, 6.0, ((2, 8), (3, 4)), jnp.float32),
        "previous": centred(arg_keys[1], (5, NZ, NX, NY), 1.0, 6.0, ((2, 8), (3, 4)), jnp.float32),
        "heights": draw_heights(jax.random.fold_in(arg_keys[6], 71), 0),
        "part_cells": draw_part_cells(jax.random.fold_in(arg_keys[6], 71), 0),
        "part_offsets": jnp.clip(1.0 * jax.random.uniform(arg_keys[4], (3, N_GX, N_GY, P_DEV), jnp.float32) ** block_levels(arg_keys[4], (3, N_GX, N_GY, P_DEV), ((1, 8), (2, 4)), -0.2, 0.2), 0.0, 1.0),
        "cross_counts": draw_cross_counts(jax.random.fold_in(arg_keys[6], 71), 0),
    }


courant = 0.9
viscosity = 0.1
prior_weight = -5.0 / 9.0
section_weight = 15.0 / 16.0


def fluid_cells(heights, levels):
    level_ids = lax.broadcasted_iota(jnp.int32, (levels,) + heights.shape, 0)
    return (level_ids >= heights[None]).astype(jnp.float32)


def advance_field(padded, velocity, fluid, time_step, prior):
    width_x = padded.shape[1] - 4
    width_y = padded.shape[2] - 4

    def along(offset):
        return padded[:, 2 + offset:2 + offset + width_x, 2:2 + width_y]

    def across(offset):
        return padded[:, 2:2 + width_x, 2 + offset:2 + offset + width_y]

    center = along(0)
    grad_x = (8.0 * (along(1) - along(-1)) - (along(2) - along(-2))) / 12.0
    grad_y = (8.0 * (across(1) - across(-1)) - (across(2) - across(-2))) / 12.0
    stacked = jnp.pad(center, ((1, 1), (0, 0), (0, 0)))
    level_up = stacked[2:]
    level_down = stacked[:-2]
    grad_z = 0.5 * (level_up - level_down)
    laplace = along(1) + along(-1) + across(1) + across(-1) + level_up + level_down - 6.0 * center
    tendency = viscosity * laplace - (velocity[0] * grad_x + velocity[1] * grad_y + velocity[2] * grad_z)
    accumulated = prior_weight * prior + tendency
    updated = center + section_weight * time_step * accumulated
    return updated * fluid, accumulated * fluid


def sample(flat_vel, level_ids, row_index, col_index, row_len, plane_len, offsets):
    anchor = level_ids * plane_len + row_index * row_len + col_index
    frac_x = offsets[0]
    frac_y = offsets[1]
    corner_a = flat_vel[:, anchor]
    corner_b = flat_vel[:, anchor + row_len]
    corner_c = flat_vel[:, anchor + 1]
    corner_d = flat_vel[:, anchor + row_len + 1]
    return ((1.0 - frac_x) * (1.0 - frac_y) * corner_a + frac_x * (1.0 - frac_y) * corner_b
            + (1.0 - frac_x) * frac_y * corner_c + frac_x * frac_y * corner_d)


def reference(fields, previous, heights, part_cells, part_offsets, cross_counts):
    wrapped = jnp.pad(fields, ((0, 0), (0, 0), (2, 2), (0, 0)), mode="wrap")
    padded = jnp.pad(wrapped, ((0, 0), (0, 0), (0, 0), (2, 2)))
    speeds = jnp.max(jnp.abs(fields[0]) + jnp.abs(fields[1]) + jnp.abs(fields[2]))
    time_step = courant / (speeds + 1e-6)
    fluid = fluid_cells(heights, NZ)
    velocity = fields[0:3]

    def one_field(pair):
        return advance_field(pair[0], velocity, fluid, time_step, pair[1])

    updated, accumulated = lax.map(one_field, (padded, previous))
    level_ids = part_cells // (CX * CY)
    row_index = (part_cells // CY) % CX + CX * lax.broadcasted_iota(jnp.int32, part_cells.shape, 0) + 2
    col_index = part_cells % CY + CY * lax.broadcasted_iota(jnp.int32, part_cells.shape, 1) + 2
    flat_vel = padded[0:3].reshape(3, -1)
    part_vel = sample(flat_vel, level_ids, row_index, col_index, NY + 4, (NX + 4) * (NY + 4), part_offsets)
    advanced = part_offsets + time_step * part_vel
    block_index = lax.broadcasted_iota(jnp.int32, (1, 1, CAP), 2)
    live_right = (block_index < cross_counts[:, :, 0:1]).astype(jnp.float32)
    live_left = (block_index < cross_counts[:, :, 1:2]).astype(jnp.float32)
    right_block = advanced[..., P_KEEP:P_KEEP + CAP] * live_right
    left_block = advanced[..., P_KEEP + CAP:] * live_left
    part_moved = jnp.concatenate([advanced[..., :P_KEEP], jnp.roll(right_block, 1, axis=1), jnp.roll(left_block, -1, axis=1)], axis=-1)
    return updated, accumulated, part_moved
```

```python
import functools

import jax
import jax.numpy as jnp
from jax import lax
from jax.experimental import pallas as pl
from jax.experimental.pallas import tpu as pltpu
from jax.sharding import PartitionSpec as P

P_KEEP = 8192
CAP = 512
LANES = 128
GROUP = 4
VMEM_BYTES = 50 * 2**20

courant = 0.9
viscosity = 0.1
prior_weight = -5.0 / 9.0
section_weight = 15.0 / 16.0

MESH = pl.DeviceIdType.MESH


def lane_ids(rows):
    return lax.broadcasted_iota(jnp.int32, (rows, LANES), 1)


def exchange_kernel(
    n_gx, n_gy, n_fields, levels, width_x,
    x_ref, low_ref, high_ref, corner_ref, cols_ref, speed_ref,
    planes, packed, from_left, from_right, speed_own, speed_row, speed_y, speed_x,
    send_sems, recv_sems, y_send, y_recv, x_send, x_recv,
):
    p = lax.axis_index("gx")
    q = lax.axis_index("gy")

    def at(dp, dq):
        return (lax.rem(p + dp + n_gx, n_gx), lax.rem(q + dq + n_gy, n_gy))

    barrier = pltpu.get_barrier_semaphore()
    peers = [at(d, 0) for d in range(1, n_gx)] + [at(0, d) for d in range(1, n_gy)]
    peers += [at(-1, -1), at(1, 1)]
    for peer in peers:
        pl.semaphore_signal(barrier, inc=1, device_id=peer, device_id_type=MESH)

    columns = n_fields * levels
    for slot, row in enumerate((0, 1, width_x - 2, width_x - 1)):
        planes[slot] = x_ref[pl.ds(row, columns, stride=width_x), :]
    pl.semaphore_wait(barrier, len(peers))

    def remote(src, dst, index, peer):
        return pltpu.make_async_remote_copy(
            src_ref=src, dst_ref=dst, send_sem=send_sems.at[index], recv_sem=recv_sems.at[index],
            device_id=peer, device_id_type=MESH,
        )

    copies = [
        remote(planes.at[pl.ds(0, 2)], high_ref, 0, at(-1, 0)),
        remote(planes.at[pl.ds(2, 2)], low_ref, 1, at(1, 0)),
        remote(planes.at[0, pl.ds(0, 3 * levels)], corner_ref, 2, at(-1, -1)),
    ]
    for copy in copies:
        copy.start()

    rows = levels * width_x

    def fastest_rows(i, best):
        start = pl.multiple_of(i * 64, 64)
        total = (
            jnp.abs(x_ref[pl.ds(start, 64), :])
            + jnp.abs(x_ref[pl.ds(rows + start, 64), :])
            + jnp.abs(x_ref[pl.ds(2 * rows + start, 64), :])
        )
        return jnp.maximum(best, jnp.max(total.reshape(8, 8, LANES), axis=0))

    speed_own[...] = lax.fori_loop(0, rows // 64, fastest_rows, jnp.zeros((8, LANES), jnp.float32))

    y_copies = []
    for d in range(1, n_gy):
        y_copies.append(
            pltpu.make_async_remote_copy(
                src_ref=speed_own, dst_ref=speed_y.at[d], send_sem=y_send.at[d], recv_sem=y_recv.at[d],
                device_id=at(0, d), device_id_type=MESH,
            )
        )
        y_copies[-1].start()

    lanes = lane_ids(width_x)
    per_pack = LANES // GROUP
    packs = columns // per_pack

    def pack(j, carry):
        total = jnp.zeros((width_x, LANES), jnp.float32)
        for i in range(per_pack):
            start = pl.multiple_of((j * per_pack + i) * width_x, width_x)
            turned = pltpu.roll(x_ref[pl.ds(start, width_x), :], (2 + GROUP * i) % LANES, 1)
            total = jnp.where(lanes // GROUP == i, turned, total)
        packed[pl.ds(pl.multiple_of(j * width_x, width_x), width_x), :] = total
        return carry

    lax.fori_loop(0, packs, pack, 0)
    side = [
        remote(packed, from_right, 3, at(0, -1)),
        remote(packed, from_left, 4, at(0, 1)),
    ]
    for copy in side:
        copy.start()

    best = speed_own[...]
    for d in range(1, n_gy):
        y_copies[d - 1].wait()
        best = jnp.maximum(best, speed_y[d])
    speed_row[...] = best
    x_copies = []
    for d in range(1, n_gx):
        x_copies.append(
            pltpu.make_async_remote_copy(
                src_ref=speed_row, dst_ref=speed_x.at[d], send_sem=x_send.at[d], recv_sem=x_recv.at[d],
                device_id=at(d, 0), device_id_type=MESH,
            )
        )
        x_copies[-1].start()

    for copy in side:
        copy.wait()
    has_left = jnp.where(q > 0, 1.0, 0.0)
    has_right = jnp.where(q < n_gy - 1, 1.0, 0.0)
    for j in range(packs):
        here = pl.ds(j * width_x, width_x)
        cols_ref[here, :] = jnp.where(
            lanes % GROUP < 2, from_left[here, :] * has_left, from_right[here, :] * has_right
        )

    for d in range(1, n_gx):
        x_copies[d - 1].wait()
        best = jnp.maximum(best, speed_x[d])
    speed_ref[...] = jnp.broadcast_to(jnp.max(best, keepdims=True), (8, LANES))
    for copy in copies:
        copy.wait()
    corner_ref[...] = corner_ref[...] * has_right


def exchange(mesh, flat, n_fields, levels, width_x):
    n_gx, n_gy = mesh.shape["gx"], mesh.shape["gy"]
    columns = n_fields * levels
    packs = columns * GROUP // LANES
    f32 = jnp.float32
    vmem = pl.BlockSpec(memory_space=pltpu.VMEM)
    shapes = [(2, columns, LANES), (2, columns, LANES), (3 * levels, LANES), (packs * width_x, LANES), (8, LANES)]
    return pl.pallas_call(
        functools.partial(exchange_kernel, n_gx, n_gy, n_fields, levels, width_x),
        out_shape=[jax.ShapeDtypeStruct(s, f32) for s in shapes],
        in_specs=[vmem],
        out_specs=[vmem] * 5,
        scratch_shapes=[
            pltpu.VMEM((4, columns, LANES), f32),
            pltpu.VMEM((packs * width_x, LANES), f32),
            pltpu.VMEM((packs * width_x, LANES), f32),
            pltpu.VMEM((packs * width_x, LANES), f32),
            pltpu.VMEM((8, LANES), f32),
            pltpu.VMEM((8, LANES), f32),
            pltpu.VMEM((n_gy, 8, LANES), f32),
            pltpu.VMEM((n_gx, 8, LANES), f32),
            pltpu.SemaphoreType.DMA((5,)),
            pltpu.SemaphoreType.DMA((5,)),
            pltpu.SemaphoreType.DMA((n_gy,)),
            pltpu.SemaphoreType.DMA((n_gy,)),
            pltpu.SemaphoreType.DMA((n_gx,)),
            pltpu.SemaphoreType.DMA((n_gx,)),
        ],
        compiler_params=pltpu.CompilerParams(
            collective_id=0, has_side_effects=True, vmem_limit_bytes=VMEM_BYTES
        ),
    )(flat)


def unpack_shift(i):
    return LANES - 2 - GROUP * i


def stencil_kernel(
    levels, width_x, x_ref, vel_ref, prior_ref, heights_ref, low_ref, high_ref, cols_ref, speed_ref,
    new_ref, acc_ref, ext,
):
    span = width_x + 16
    per_pack = LANES // GROUP
    step = section_weight * (courant / (speed_ref[0:1, :] + 1e-06))
    zero = jnp.zeros((span, LANES), jnp.float32)
    ext[0:span, :] = zero
    ext[(levels + 1) * span : (levels + 2) * span, :] = zero

    def fill(k, carry):
        start = pl.multiple_of((k + 1) * span + 8, 8)
        ext[pl.ds(start, width_x), :] = x_ref[0, k]
        return carry

    lax.fori_loop(0, levels, fill, 0, unroll=8)
    for d in range(2):
        ext[pl.ds(span + 6 + d, levels, stride=span), :] = low_ref[d]
        ext[pl.ds(span + 8 + width_x + d, levels, stride=span), :] = high_ref[d]
    lanes = lane_ids(width_x)
    heights = heights_ref[...]

    def level(k):
        base = pl.multiple_of((k + 1) * span, 8)
        center = ext[pl.ds(base + 8, width_x), :]

        def along(d):
            return ext[pl.ds(base + 8 + d, width_x), :]

        up = ext[pl.ds(base + span + 8, width_x), :]
        down = ext[pl.ds(base - span + 8, width_x), :]
        edge = cols_ref[0, k // per_pack]
        edge = pltpu.roll(edge, unpack_shift(lax.rem(k, per_pack)), 1)
        right1 = pltpu.roll(jnp.where(lanes == 0, edge, center), LANES - 1, 1)
        right2 = pltpu.roll(jnp.where(lanes <= 1, edge, center), LANES - 2, 1)
        left1 = pltpu.roll(jnp.where(lanes == LANES - 1, edge, center), 1, 1)
        left2 = pltpu.roll(jnp.where(lanes >= LANES - 2, edge, center), 2, 1)
        low1, high1 = along(-1), along(1)
        grad_x = (high1 - low1) * (8.0 / 12.0) - (along(2) - along(-2)) * (1.0 / 12.0)
        grad_y = (right1 - left1) * (8.0 / 12.0) - (right2 - left2) * (1.0 / 12.0)
        grad_z = 0.5 * (up - down)
        laplace = high1 + low1 + right1 + left1 + up + down - 6.0 * center
        tendency = viscosity * laplace - (
            vel_ref[0, k] * grad_x + vel_ref[1, k] * grad_y + vel_ref[2, k] * grad_z
        )
        acc = prior_weight * prior_ref[0, k] + tendency
        fluid = k >= heights
        acc_ref[0, k] = jnp.where(fluid, acc, 0.0)
        new_ref[0, k] = jnp.where(fluid, center + step * acc, 0.0)

    def some(i, carry):
        for j in range(4):
            level(i * 4 + j)
        return carry

    lax.fori_loop(0, levels // 4, some, 0)


def stencil(fields, previous, heights, low, high, cols, speed):
    n_fields, levels, width_x, width_y = fields.shape
    halves = levels * GROUP // LANES
    block = pl.BlockSpec((1, levels, width_x, width_y), lambda f: (f, 0, 0, 0))
    return pl.pallas_call(
        functools.partial(stencil_kernel, levels, width_x),
        grid=(n_fields,),
        out_shape=[jax.ShapeDtypeStruct(fields.shape, jnp.float32)] * 2,
        in_specs=[
            block,
            pl.BlockSpec((3, levels, width_x, width_y), lambda f: (0, 0, 0, 0)),
            block,
            pl.BlockSpec((width_x, width_y), lambda f: (0, 0)),
            pl.BlockSpec((2, levels, LANES), lambda f: (0, f, 0)),
            pl.BlockSpec((2, levels, LANES), lambda f: (0, f, 0)),
            pl.BlockSpec((1, halves, width_x, LANES), lambda f: (f, 0, 0, 0)),
            pl.BlockSpec((8, LANES), lambda f: (0, 0)),
        ],
        out_specs=[block, block],
        scratch_shapes=[pltpu.VMEM(((levels + 2) * (width_x + 16), LANES), jnp.float32)],
        compiler_params=pltpu.CompilerParams(vmem_limit_bytes=VMEM_BYTES),
    )(fields, fields, previous, heights, low, high, cols.reshape(n_fields, halves, width_x, LANES), speed)


def particle_kernel(
    levels, width_x, blocks, tile_ref, col_ref, off_ref, x_ref, high_ref, corner_ref, cols_ref, speed_ref,
    out_ref, table,
):
    per_pack = LANES // GROUP
    lanes = lane_ids(width_x)
    tiles = levels * width_x

    def build(k, carry):
        pack = pl.multiple_of(k // per_pack * width_x, 8)
        base = pl.multiple_of((k * width_x + 1) * 8, 8)
        for s in range(3):
            own = x_ref[s, k]
            edge = cols_ref[pl.ds(s * (levels // per_pack) * width_x + pack, width_x), :]
            edge = pltpu.roll(edge, unpack_shift(lax.rem(k, per_pack)), 1)
            turned = jnp.where(lanes == 0, edge, own)
            table[pl.ds(base + s, width_x, stride=8), :] = own
            table[pl.ds(base - 8 + 3 + s, width_x, stride=8), :] = own
            table[pl.ds(tiles * 8 + base + s, width_x, stride=8), :] = turned
            table[pl.ds(tiles * 8 + base - 8 + 3 + s, width_x, stride=8), :] = turned
        return carry

    lax.fori_loop(0, levels, build, 0)
    first = lane_ids(levels) == 0
    for s in range(3):
        plane = high_ref[0, s * levels : (s + 1) * levels, :]
        corner = corner_ref[s * levels : (s + 1) * levels, :]
        table[pl.ds(width_x * 8 + 3 + s, levels, stride=width_x * 8), :] = plane
        table[pl.ds((tiles + width_x) * 8 + 3 + s, levels, stride=width_x * 8), :] = jnp.where(
            first, corner, plane
        )

    half = LANES // 2
    lanes = lane_ids(8)
    sub = lax.broadcasted_iota(jnp.int32, (8, LANES), 0)
    time_step = courant / (speed_ref[0:1, :] + 1e-06)
    place = lanes % half

    def one(j, carry):
        sums = []
        for h in range(2):
            ids = jnp.broadcast_to(col_ref[pl.ds(2 * j + h, 1), :], (8, LANES))
            got = jnp.zeros((8, LANES), jnp.float32)
            for i in range(half):
                start = pl.multiple_of(tile_ref[j * LANES + h * half + i], 8)
                tile = table[pl.ds(start, 8), :]
                turned = jnp.take_along_axis(tile, ids, axis=1, mode="promise_in_bounds")
                got = jnp.where(place == i, turned, got)
            frac = off_ref[1, pl.ds(j, 1), :]
            other = pltpu.roll(frac, half, 1)
            if h == 0:
                weight = jnp.where(lanes[0:1] < half, 1.0 - frac, other)
            else:
                weight = jnp.where(lanes[0:1] < half, 1.0 - other, frac)
            got = got * weight
            sums.append(got + pltpu.roll(got, half, 1))
        both = jnp.where(lanes < half, sums[0], sums[1])
        frac = off_ref[0, pl.ds(j, 1), :]
        both = both * jnp.where(sub < 3, 1.0 - frac, frac)
        vel = both[0:3] + both[3:6]
        for s in range(3):
            out_ref[s, pl.ds(j, 1), :] = off_ref[s, pl.ds(j, 1), :] + time_step * vel[s : s + 1]
        return carry

    lax.fori_loop(0, blocks, one, 0)


def particles(fields, cells, offsets, high, corner, cols, speed):
    levels, width_x, width_y = fields.shape[1:]
    total = cells.shape[0]
    blocks = total // LANES
    half = LANES // 2
    column = cells % width_y
    tile = (cells // width_y + 1 + jnp.where(column == width_y - 1, levels * width_x, 0)) * 8
    pairs = column.reshape(-1, half)
    pairs = jnp.concatenate([pairs, (pairs + 1) % width_y], axis=1)
    vmem = pl.BlockSpec(memory_space=pltpu.VMEM)
    return pl.pallas_call(
        functools.partial(particle_kernel, levels, width_x, blocks),
        grid=(1,),
        out_shape=jax.ShapeDtypeStruct((3, blocks, LANES), jnp.float32),
        in_specs=[
            pl.BlockSpec(memory_space=pltpu.SMEM),
            vmem,
            vmem,
            pl.BlockSpec((3, levels, width_x, width_y), lambda i: (0, 0, 0, 0)),
            vmem,
            vmem,
            vmem,
            vmem,
        ],
        out_specs=vmem,
        scratch_shapes=[pltpu.VMEM(((2 * levels * width_x + 1) * 8, LANES), jnp.float32)],
        compiler_params=pltpu.CompilerParams(vmem_limit_bytes=VMEM_BYTES),
    )(tile, pairs, offsets.reshape(3, blocks, LANES), fields, high, corner, cols, speed)


def local(mesh, fields, previous, heights, part_cells, part_offsets, cross_counts):
    n_fields, levels, width_x, width_y = fields.shape
    flat = fields.reshape(n_fields * levels * width_x, width_y)
    low, high, corner, cols, speed = exchange(mesh, flat, n_fields, levels, width_x)
    offsets = part_offsets[:, 0, 0]
    counts = cross_counts[0, 0]
    advanced = particles(fields, part_cells[0, 0], offsets, high, corner, cols, speed).reshape(3, -1)
    slots = lax.broadcasted_iota(jnp.int32, (CAP,), 0)
    right_block = advanced[:, P_KEEP : P_KEEP + CAP] * (slots < counts[0]).astype(jnp.float32)
    left_block = advanced[:, P_KEEP + CAP :] * (slots < counts[1]).astype(jnp.float32)
    n_gx = mesh.shape["gx"]
    from_left = lax.ppermute(right_block, "gx", [(i, (i + 1) % n_gx) for i in range(n_gx)])
    from_right = lax.ppermute(left_block, "gx", [((i + 1) % n_gx, i) for i in range(n_gx)])
    updated, accumulated = stencil(fields, previous, heights, low, high, cols, speed)
    part_moved = jnp.concatenate([advanced[:, :P_KEEP], from_left, from_right], axis=-1)
    return (updated, accumulated, part_moved.reshape(3, 1, 1, -1))


def solution(mesh):
    placed = (
        P(None, None, "gx", "gy"),
        P(None, None, "gx", "gy"),
        P("gx", "gy"),
        P("gx", "gy", None),
        P(None, "gx", "gy", None),
        P("gx", "gy", None),
    )
    return jax.shard_map(
        functools.partial(local, mesh),
        mesh=mesh,
        in_specs=placed,
        out_specs=(P(None, None, "gx", "gy"), P(None, None, "gx", "gy"), P(None, "gx", "gy", None)),
        check_vma=False,
    )
```

```python
import functools

import jax
import jax.numpy as jnp
from jax import lax
from jax.experimental import pallas as pl
from jax.experimental.pallas import tpu as pltpu
from jax.sharding import PartitionSpec as P

P_KEEP = 8192
CAP = 512
LANES = 128
GROUP = 4
VMEM_BYTES = 50 * 2**20

courant = 0.9
viscosity = 0.1
prior_weight = -5.0 / 9.0
section_weight = 15.0 / 16.0

MESH = pl.DeviceIdType.MESH


def lane_ids(rows):
    return lax.broadcasted_iota(jnp.int32, (rows, LANES), 1)


def unpack_shift(i):
    return LANES - 2 - GROUP * i


def advance_kernel(
    n_gx, n_gy, n_fields, levels, width_x, blocks,
    tile_ref, counts_ref, col_ref, off_ref, x_hbm,
    low_ref, high_ref, cols_ref, speed_ref, out_ref,
    x_ref, table, planes, corner_ref, packed, from_left, from_right, speed_own, speed_row, speed_y, speed_x,
    cross_own, cross_in,
    load_sem, send_sems, recv_sems, y_send, y_recv, x_send, x_recv,
):
    p = lax.axis_index("gx")
    q = lax.axis_index("gy")

    def at(dp, dq):
        return (lax.rem(p + dp + n_gx, n_gx), lax.rem(q + dq + n_gy, n_gy))

    load = pltpu.make_async_copy(x_hbm, x_ref, load_sem)
    load.start()
    barrier = pltpu.get_barrier_semaphore()
    peers = [at(d, 0) for d in range(1, n_gx)] + [at(0, d) for d in range(1, n_gy)]
    peers += [at(-1, -1), at(1, 1)]
    for peer in peers:
        pl.semaphore_signal(barrier, inc=1, device_id=peer, device_id_type=MESH)

    columns = n_fields * levels
    load.wait()
    for slot, row in enumerate((0, 1, width_x - 2, width_x - 1)):
        planes[slot] = x_ref[pl.ds(row, columns, stride=width_x), :]
    pl.semaphore_wait(barrier, len(peers))

    def remote(src, dst, index, peer):
        return pltpu.make_async_remote_copy(
            src_ref=src, dst_ref=dst, send_sem=send_sems.at[index], recv_sem=recv_sems.at[index],
            device_id=peer, device_id_type=MESH,
        )

    used = 3 * levels
    near = [
        remote(planes.at[0, pl.ds(0, used)], high_ref.at[0, pl.ds(0, used)], 0, at(-1, 0)),
        remote(planes.at[0, pl.ds(0, used)], corner_ref, 1, at(-1, -1)),
    ]
    for copy in near:
        copy.start()

    rows = levels * width_x

    def fastest_rows(i, best):
        start = pl.multiple_of(i * 64, 64)
        total = (
            jnp.abs(x_ref[pl.ds(start, 64), :])
            + jnp.abs(x_ref[pl.ds(rows + start, 64), :])
            + jnp.abs(x_ref[pl.ds(2 * rows + start, 64), :])
        )
        return jnp.maximum(best, jnp.max(total.reshape(8, 8, LANES), axis=0))

    speed_own[...] = lax.fori_loop(0, rows // 64, fastest_rows, jnp.zeros((8, LANES), jnp.float32))

    y_copies = []
    for d in range(1, n_gy):
        y_copies.append(
            pltpu.make_async_remote_copy(
                src_ref=speed_own, dst_ref=speed_y.at[d], send_sem=y_send.at[d], recv_sem=y_recv.at[d],
                device_id=at(0, d), device_id_type=MESH,
            )
        )
        y_copies[-1].start()

    lanes = lane_ids(width_x)
    per_pack = LANES // GROUP
    packs = columns // per_pack

    def pack(j, carry):
        total = jnp.zeros((width_x, LANES), jnp.float32)
        for i in range(per_pack):
            start = pl.multiple_of((j * per_pack + i) * width_x, width_x)
            turned = pltpu.roll(x_ref[pl.ds(start, width_x), :], (2 + GROUP * i) % LANES, 1)
            total = jnp.where(lanes // GROUP == i, turned, total)
        packed[pl.ds(pl.multiple_of(j * width_x, width_x), width_x), :] = total
        return carry

    lax.fori_loop(0, packs, pack, 0)
    side = [
        remote(packed, from_right, 2, at(0, -1)),
        remote(packed, from_left, 3, at(0, 1)),
    ]
    for copy in side:
        copy.start()
    rest = columns - used
    far = [
        remote(planes.at[0, pl.ds(used, rest)], high_ref.at[0, pl.ds(used, rest)], 4, at(-1, 0)),
        remote(planes.at[1], high_ref.at[1], 5, at(-1, 0)),
        remote(planes.at[pl.ds(2, 2)], low_ref, 6, at(1, 0)),
    ]

    best = speed_own[...]
    for d in range(1, n_gy):
        y_copies[d - 1].wait()
        best = jnp.maximum(best, speed_y[d])
    speed_row[...] = best
    x_copies = []
    for d in range(1, n_gx):
        x_copies.append(
            pltpu.make_async_remote_copy(
                src_ref=speed_row, dst_ref=speed_x.at[d], send_sem=x_send.at[d], recv_sem=x_recv.at[d],
                device_id=at(d, 0), device_id_type=MESH,
            )
        )
        x_copies[-1].start()
    for copy in far:
        copy.start()

    def build_own(k, carry):
        base = k * width_x + 1
        for s in range(3):
            own = x_ref[pl.ds(pl.multiple_of(s * rows + k * width_x, 8), width_x), :]
            table[pl.ds(base, width_x), s, :] = own
            table[pl.ds(base - 1, width_x), 3 + s, :] = own
        return carry

    lax.fori_loop(0, levels, build_own, 0, unroll=2)

    for copy in side:
        copy.wait()
    has_left = jnp.where(q > 0, 1.0, 0.0)
    has_right = jnp.where(q < n_gy - 1, 1.0, 0.0)
    for j in range(packs):
        here = pl.ds(j * width_x, width_x)
        cols_ref[here, :] = jnp.where(
            lanes % GROUP < 2, from_left[here, :] * has_left, from_right[here, :] * has_right
        )

    def build_turned(j, carry):
        for i in range(per_pack):
            k = j * per_pack + i
            base = k * width_x + 1 + rows
            for s in range(3):
                own = x_ref[pl.ds(pl.multiple_of(s * rows + k * width_x, 8), width_x), :]
                start = pl.multiple_of((s * (levels // per_pack) + j) * width_x, 8)
                edge = pltpu.roll(cols_ref[pl.ds(start, width_x), :], unpack_shift(i), 1)
                turned = jnp.where(lanes == 0, edge, own)
                table[pl.ds(base, width_x), s, :] = turned
                table[pl.ds(base - 1, width_x), 3 + s, :] = turned
        return carry

    lax.fori_loop(0, levels // per_pack, build_turned, 0)
    for copy in near:
        copy.wait()
    first = lane_ids(levels) == 0
    for s in range(3):
        plane = high_ref[0, s * levels : (s + 1) * levels, :]
        corner = corner_ref[s * levels : (s + 1) * levels, :] * has_right
        table[pl.ds(width_x, levels, stride=width_x), 3 + s, :] = plane
        table[pl.ds(rows + width_x, levels, stride=width_x), 3 + s, :] = jnp.where(
            first, corner, plane
        )

    for d in range(1, n_gx):
        x_copies[d - 1].wait()
        best = jnp.maximum(best, speed_x[d])
    fastest = jnp.broadcast_to(jnp.max(best, keepdims=True), (8, LANES))
    speed_ref[...] = fastest
    time_step = courant / (fastest[0:1, :] + 1e-06)

    half = LANES // 2
    lanes = lane_ids(8)
    sub = lax.broadcasted_iota(jnp.int32, (8, LANES), 0)
    place = lanes % half

    def one(j, carry):
        sums = []
        for h in range(2):
            ids = jnp.broadcast_to(col_ref[pl.ds(2 * j + h, 1), :], (8, LANES))
            got = jnp.zeros((8, LANES), jnp.float32)
            for i in range(half):
                tile = table[tile_ref[j * LANES + h * half + i]]
                turned = jnp.take_along_axis(tile, ids, axis=1, mode="promise_in_bounds")
                got = jnp.where(place == i, turned, got)
            frac = off_ref[1, pl.ds(j, 1), :]
            other = pltpu.roll(frac, half, 1)
            if h == 0:
                weight = jnp.where(lanes[0:1] < half, 1.0 - frac, other)
            else:
                weight = jnp.where(lanes[0:1] < half, 1.0 - other, frac)
            got = got * weight
            sums.append(got + pltpu.roll(got, half, 1))
        both = jnp.where(lanes < half, sums[0], sums[1])
        frac = off_ref[0, pl.ds(j, 1), :]
        both = both * jnp.where(sub < 3, 1.0 - frac, frac)
        vel = both[0:3] + both[3:6]
        for s in range(3):
            out_ref[s, pl.ds(j, 1), :] = off_ref[s, pl.ds(j, 1), :] + time_step * vel[s : s + 1]
        return carry

    kept, cap = P_KEEP // LANES, CAP // LANES
    lax.fori_loop(kept, blocks, one, 0)
    slots = lax.broadcasted_iota(jnp.int32, (cap, LANES), 0) * LANES + lane_ids(cap)
    crossing = []
    for way in range(2):
        live = jnp.where(slots < counts_ref[way], 1.0, 0.0)
        for s in range(3):
            cross_own[way, s] = out_ref[s, pl.ds(kept + way * cap, cap), :] * live
        crossing.append(remote(cross_own.at[way], cross_in.at[way], 7 + way, at(1 - 2 * way, 0)))
        crossing[-1].start()
    lax.fori_loop(0, kept, one, 0)
    for way in range(2):
        crossing[way].wait()
        for s in range(3):
            out_ref[s, pl.ds(kept + way * cap, cap), :] = cross_in[way, s]
    for copy in far:
        copy.wait()


def advance(mesh, fields, cells, offsets, counts):
    n_gx, n_gy = mesh.shape["gx"], mesh.shape["gy"]
    n_fields, levels, width_x, width_y = fields.shape
    columns = n_fields * levels
    packed = (columns * GROUP // LANES * width_x, LANES)
    blocks = cells.shape[0] // LANES
    half = LANES // 2
    column = cells % width_y
    tile = cells // width_y + 1 + jnp.where(column == width_y - 1, levels * width_x, 0)
    pairs = column.reshape(-1, half)
    pairs = jnp.concatenate([pairs, (pairs + 1) % width_y], axis=1)
    f32 = jnp.float32
    vmem = pl.BlockSpec(memory_space=pltpu.VMEM)
    smem = pl.BlockSpec(memory_space=pltpu.SMEM)
    shapes = [(2, columns, LANES), (2, columns, LANES), packed, (8, LANES), (3, blocks, LANES)]
    return pl.pallas_call(
        functools.partial(advance_kernel, n_gx, n_gy, n_fields, levels, width_x, blocks),
        out_shape=[jax.ShapeDtypeStruct(s, f32) for s in shapes],
        in_specs=[smem, smem, vmem, vmem, pl.BlockSpec(memory_space=pl.ANY)],
        out_specs=[vmem] * 5,
        scratch_shapes=[
            pltpu.VMEM((columns * width_x, LANES), f32),
            pltpu.VMEM((2 * levels * width_x + 1, 8, LANES), f32),
            pltpu.VMEM((4, columns, LANES), f32),
            pltpu.VMEM((3 * levels, LANES), f32),
            pltpu.VMEM(packed, f32),
            pltpu.VMEM(packed, f32),
            pltpu.VMEM(packed, f32),
            pltpu.VMEM((8, LANES), f32),
            pltpu.VMEM((8, LANES), f32),
            pltpu.VMEM((n_gy, 8, LANES), f32),
            pltpu.VMEM((n_gx, 8, LANES), f32),
            pltpu.VMEM((2, 3, CAP // LANES, LANES), f32),
            pltpu.VMEM((2, 3, CAP // LANES, LANES), f32),
            pltpu.SemaphoreType.DMA,
            pltpu.SemaphoreType.DMA((9,)),
            pltpu.SemaphoreType.DMA((9,)),
            pltpu.SemaphoreType.DMA((n_gy,)),
            pltpu.SemaphoreType.DMA((n_gy,)),
            pltpu.SemaphoreType.DMA((n_gx,)),
            pltpu.SemaphoreType.DMA((n_gx,)),
        ],
        compiler_params=pltpu.CompilerParams(
            collective_id=0, has_side_effects=True, vmem_limit_bytes=VMEM_BYTES
        ),
    )(tile, counts, pairs, offsets.reshape(3, blocks, LANES), fields.reshape(-1, width_y))


def stencil_kernel(
    levels, width_x, x_ref, vel_ref, prior_ref, heights_ref, low_ref, high_ref, cols_ref, speed_ref,
    new_ref, acc_ref, ext,
):
    span = width_x + 16
    per_pack = LANES // GROUP
    step = section_weight * (courant / (speed_ref[0:1, :] + 1e-06))
    zero = jnp.zeros((span, LANES), jnp.float32)
    ext[0:span, :] = zero
    ext[(levels + 1) * span : (levels + 2) * span, :] = zero

    def fill(k, carry):
        start = pl.multiple_of((k + 1) * span + 8, 8)
        ext[pl.ds(start, width_x), :] = x_ref[0, k]
        return carry

    lax.fori_loop(0, levels, fill, 0, unroll=8)
    for d in range(2):
        ext[pl.ds(span + 6 + d, levels, stride=span), :] = low_ref[d]
        ext[pl.ds(span + 8 + width_x + d, levels, stride=span), :] = high_ref[d]
    lanes = lane_ids(width_x)
    heights = heights_ref[...]

    def level(half, i):
        k = half * per_pack + i
        base = pl.multiple_of((k + 1) * span, 8)
        center = ext[pl.ds(base + 8, width_x), :]

        def along(d):
            return ext[pl.ds(base + 8 + d, width_x), :]

        up = ext[pl.ds(base + span + 8, width_x), :]
        down = ext[pl.ds(base - span + 8, width_x), :]
        edge = pltpu.roll(cols_ref[0, half], unpack_shift(i), 1)
        right1 = pltpu.roll(jnp.where(lanes == 0, edge, center), LANES - 1, 1)
        right2 = pltpu.roll(jnp.where(lanes <= 1, edge, center), LANES - 2, 1)
        left1 = pltpu.roll(jnp.where(lanes == LANES - 1, edge, center), 1, 1)
        left2 = pltpu.roll(jnp.where(lanes >= LANES - 2, edge, center), 2, 1)
        low1, high1 = along(-1), along(1)
        grad_x = (high1 - low1) * (8.0 / 12.0) - (along(2) - along(-2)) * (1.0 / 12.0)
        grad_y = (right1 - left1) * (8.0 / 12.0) - (right2 - left2) * (1.0 / 12.0)
        grad_z = 0.5 * (up - down)
        laplace = high1 + low1 + right1 + left1 + up + down - 6.0 * center
        tendency = viscosity * laplace - (
            vel_ref[0, k] * grad_x + vel_ref[1, k] * grad_y + vel_ref[2, k] * grad_z
        )
        acc = prior_weight * prior_ref[0, k] + tendency
        fluid = k >= heights
        acc_ref[0, k] = jnp.where(fluid, acc, 0.0)
        new_ref[0, k] = jnp.where(fluid, center + step * acc, 0.0)

    def some(half, carry):
        for i in range(per_pack):
            level(half, i)
        return carry

    lax.fori_loop(0, levels // per_pack, some, 0)


def stencil(fields, previous, heights, low, high, cols, speed):
    n_fields, levels, width_x, width_y = fields.shape
    halves = levels * GROUP // LANES
    block = pl.BlockSpec((1, levels, width_x, width_y), lambda f: (f, 0, 0, 0))
    return pl.pallas_call(
        functools.partial(stencil_kernel, levels, width_x),
        grid=(n_fields,),
        out_shape=[jax.ShapeDtypeStruct(fields.shape, jnp.float32)] * 2,
        in_specs=[
            block,
            pl.BlockSpec((3, levels, width_x, width_y), lambda f: (0, 0, 0, 0)),
            block,
            pl.BlockSpec((width_x, width_y), lambda f: (0, 0)),
            pl.BlockSpec((2, levels, LANES), lambda f: (0, f, 0)),
            pl.BlockSpec((2, levels, LANES), lambda f: (0, f, 0)),
            pl.BlockSpec((1, halves, width_x, LANES), lambda f: (f, 0, 0, 0)),
            pl.BlockSpec((8, LANES), lambda f: (0, 0)),
        ],
        out_specs=[block, block],
        scratch_shapes=[pltpu.VMEM(((levels + 2) * (width_x + 16), LANES), jnp.float32)],
        compiler_params=pltpu.CompilerParams(vmem_limit_bytes=VMEM_BYTES),
    )(fields, fields, previous, heights, low, high, cols.reshape(n_fields, halves, width_x, LANES), speed)


def local(mesh, fields, previous, heights, part_cells, part_offsets, cross_counts):
    low, high, cols, speed, moved = advance(
        mesh, fields, part_cells[0, 0], part_offsets[:, 0, 0], cross_counts[0, 0]
    )
    updated, accumulated = stencil(fields, previous, heights, low, high, cols, speed)
    return (updated, accumulated, moved.reshape(3, 1, 1, -1))


def solution(mesh):
    placed = (
        P(None, None, "gx", "gy"),
        P(None, None, "gx", "gy"),
        P("gx", "gy"),
        P("gx", "gy", None),
        P(None, "gx", "gy", None),
        P("gx", "gy", None),
    )
    return jax.shard_map(
        functools.partial(local, mesh),
        mesh=mesh,
        in_specs=placed,
        out_specs=(P(None, None, "gx", "gy"), P(None, None, "gx", "gy"), P(None, "gx", "gy", None)),
        check_vma=False,
    )
```

```python
import functools

import jax
import jax.numpy as jnp
from jax import lax
from jax.experimental import pallas as pl
from jax.experimental.pallas import tpu as pltpu
from jax.sharding import PartitionSpec as P

P_KEEP = 8192
CAP = 512
LANES = 128
GROUP = 4
VMEM_BYTES = 60 * 2**20

courant = 0.9
viscosity = 0.1
prior_weight = -5.0 / 9.0
section_weight = 15.0 / 16.0

MESH = pl.DeviceIdType.MESH


def lane_ids(rows):
    return lax.broadcasted_iota(jnp.int32, (rows, LANES), 1)


def unpack_shift(i):
    return LANES - 2 - GROUP * i


def advance_kernel(
    n_gx, n_gy, n_fields, levels, width_x, blocks,
    tile_ref, counts_ref, cell_ref, off_ref, x_hbm,
    low_ref, high_ref, cols_ref, speed_ref, out_ref,
    x_ref, table, planes, corner_ref, packed, from_left, from_right, speed_own, speed_row, speed_y, speed_x,
    cross_own, cross_in,
    load_sem, send_sems, recv_sems, y_send, y_recv, x_send, x_recv,
):
    p = lax.axis_index("gx")
    q = lax.axis_index("gy")

    def at(dp, dq):
        return (lax.rem(p + dp + n_gx, n_gx), lax.rem(q + dq + n_gy, n_gy))

    load = pltpu.make_async_copy(x_hbm, x_ref, load_sem)
    load.start()
    barrier = pltpu.get_barrier_semaphore()
    peers = [at(d, 0) for d in range(1, n_gx)] + [at(0, d) for d in range(1, n_gy)]
    peers += [at(-1, -1), at(1, 1)]
    for peer in peers:
        pl.semaphore_signal(barrier, inc=1, device_id=peer, device_id_type=MESH)

    columns = n_fields * levels
    load.wait()
    for slot, row in enumerate((0, 1, width_x - 2, width_x - 1)):
        planes[slot] = x_ref[pl.ds(row, columns, stride=width_x), :]
    pl.semaphore_wait(barrier, len(peers))

    def remote(src, dst, index, peer):
        return pltpu.make_async_remote_copy(
            src_ref=src, dst_ref=dst, send_sem=send_sems.at[index], recv_sem=recv_sems.at[index],
            device_id=peer, device_id_type=MESH,
        )

    used = 3 * levels
    near = [
        remote(planes.at[0, pl.ds(0, used)], high_ref.at[0, pl.ds(0, used)], 0, at(-1, 0)),
        remote(planes.at[0, pl.ds(0, used)], corner_ref, 1, at(-1, -1)),
    ]
    for copy in near:
        copy.start()

    rows = levels * width_x

    def fastest_rows(i, best):
        start = pl.multiple_of(i * 64, 64)
        total = (
            jnp.abs(x_ref[pl.ds(start, 64), :])
            + jnp.abs(x_ref[pl.ds(rows + start, 64), :])
            + jnp.abs(x_ref[pl.ds(2 * rows + start, 64), :])
        )
        return jnp.maximum(best, jnp.max(total.reshape(8, 8, LANES), axis=0))

    speed_own[...] = lax.fori_loop(0, rows // 64, fastest_rows, jnp.zeros((8, LANES), jnp.float32))

    y_copies = []
    for d in range(1, n_gy):
        y_copies.append(
            pltpu.make_async_remote_copy(
                src_ref=speed_own, dst_ref=speed_y.at[d], send_sem=y_send.at[d], recv_sem=y_recv.at[d],
                device_id=at(0, d), device_id_type=MESH,
            )
        )
        y_copies[-1].start()

    lanes = lane_ids(width_x)
    per_pack = LANES // GROUP
    packs = columns // per_pack

    def pack(j, carry):
        total = jnp.zeros((width_x, LANES), jnp.float32)
        for i in range(per_pack):
            start = pl.multiple_of((j * per_pack + i) * width_x, width_x)
            turned = pltpu.roll(x_ref[pl.ds(start, width_x), :], (2 + GROUP * i) % LANES, 1)
            total = jnp.where(lanes // GROUP == i, turned, total)
        packed[pl.ds(pl.multiple_of(j * width_x, width_x), width_x), :] = total
        return carry

    lax.fori_loop(0, packs, pack, 0)
    side = [
        remote(packed, from_right, 2, at(0, -1)),
        remote(packed, from_left, 3, at(0, 1)),
    ]
    for copy in side:
        copy.start()
    rest = columns - used
    far = [
        remote(planes.at[0, pl.ds(used, rest)], high_ref.at[0, pl.ds(used, rest)], 4, at(-1, 0)),
        remote(planes.at[1], high_ref.at[1], 5, at(-1, 0)),
        remote(planes.at[pl.ds(2, 2)], low_ref, 6, at(1, 0)),
    ]

    best = speed_own[...]
    for d in range(1, n_gy):
        y_copies[d - 1].wait()
        best = jnp.maximum(best, speed_y[d])
    speed_row[...] = best
    x_copies = []
    for d in range(1, n_gx):
        x_copies.append(
            pltpu.make_async_remote_copy(
                src_ref=speed_row, dst_ref=speed_x.at[d], send_sem=x_send.at[d], recv_sem=x_recv.at[d],
                device_id=at(d, 0), device_id_type=MESH,
            )
        )
        x_copies[-1].start()
    for copy in far:
        copy.start()

    def build_own(k, carry):
        base = k * width_x + 1
        for s in range(3):
            own = x_ref[pl.ds(pl.multiple_of(s * rows + k * width_x, 8), width_x), :]
            table[pl.ds(base, width_x), s, :] = own
            table[pl.ds(base - 1, width_x), 3 + s, :] = own
        return carry

    lax.fori_loop(0, levels, build_own, 0, unroll=2)

    for copy in side:
        copy.wait()
    has_left = jnp.where(q > 0, 1.0, 0.0)
    has_right = jnp.where(q < n_gy - 1, 1.0, 0.0)
    for j in range(packs):
        here = pl.ds(j * width_x, width_x)
        cols_ref[here, :] = jnp.where(
            lanes % GROUP < 2, from_left[here, :] * has_left, from_right[here, :] * has_right
        )

    def build_turned(j, carry):
        for i in range(per_pack):
            k = j * per_pack + i
            base = k * width_x + 1 + rows
            for s in range(3):
                own = x_ref[pl.ds(pl.multiple_of(s * rows + k * width_x, 8), width_x), :]
                start = pl.multiple_of((s * (levels // per_pack) + j) * width_x, 8)
                edge = pltpu.roll(cols_ref[pl.ds(start, width_x), :], unpack_shift(i), 1)
                turned = jnp.where(lanes == 0, edge, own)
                table[pl.ds(base, width_x), s, :] = turned
                table[pl.ds(base - 1, width_x), 3 + s, :] = turned
        return carry

    lax.fori_loop(0, levels // per_pack, build_turned, 0)
    for copy in near:
        copy.wait()
    first = lane_ids(levels) == 0
    for s in range(3):
        plane = high_ref[0, s * levels : (s + 1) * levels, :]
        corner = corner_ref[s * levels : (s + 1) * levels, :] * has_right
        table[pl.ds(width_x, levels, stride=width_x), 3 + s, :] = plane
        table[pl.ds(rows + width_x, levels, stride=width_x), 3 + s, :] = jnp.where(
            first, corner, plane
        )

    for d in range(1, n_gx):
        x_copies[d - 1].wait()
        best = jnp.maximum(best, speed_x[d])
    fastest = jnp.broadcast_to(jnp.max(best, keepdims=True), (8, LANES))
    speed_ref[...] = fastest
    time_step = courant / (fastest[0:1, :] + 1e-06)

    half = LANES // 2
    lanes = lane_ids(8)
    sub = lax.broadcasted_iota(jnp.int32, (8, LANES), 0)
    place = lanes % half

    def one(j, carry):
        sums = []
        here = pl.ds(pl.multiple_of(j * LANES, LANES), LANES)
        column = cell_ref[0, :, here] % LANES
        column_other = pltpu.roll(column, half, 1)
        frac = off_ref[1, 0, :, here]
        other = pltpu.roll(frac, half, 1)
        early = lanes[0:1] < half
        for h in range(2):
            if h == 0:
                ids = jnp.where(early, column, (column_other + 1) % LANES)
                weight = jnp.where(early, 1.0 - frac, other)
            else:
                ids = jnp.where(early, column_other, (column + 1) % LANES)
                weight = jnp.where(early, 1.0 - other, frac)
            ids = jnp.broadcast_to(ids, (8, LANES))
            got = jnp.zeros((8, LANES), jnp.float32)
            for i in range(half):
                tile = table[tile_ref[0, 0, j * LANES + h * half + i]]
                turned = jnp.take_along_axis(tile, ids, axis=1, mode="promise_in_bounds")
                got = jnp.where(place == i, turned, got)
            got = got * weight
            sums.append(got + pltpu.roll(got, half, 1))
        both = jnp.where(lanes < half, sums[0], sums[1])
        frac = off_ref[0, 0, :, here]
        both = both * jnp.where(sub < 3, 1.0 - frac, frac)
        vel = both[0:3] + both[3:6]
        for s in range(3):
            out_ref[s, 0, :, here] = off_ref[s, 0, :, here] + time_step * vel[s : s + 1]
        return carry

    kept = P_KEEP // LANES
    lax.fori_loop(kept, blocks, one, 0)
    slots = lax.broadcasted_iota(jnp.int32, (1, CAP), 1)
    crossing = []
    for way in range(2):
        live = jnp.where(slots < counts_ref[0, 0, way], 1.0, 0.0)
        for s in range(3):
            cross_own[way, s] = out_ref[s, 0, :, pl.ds(P_KEEP + way * CAP, CAP)] * live
        crossing.append(remote(cross_own.at[way], cross_in.at[way], 7 + way, at(1 - 2 * way, 0)))
        crossing[-1].start()
    lax.fori_loop(0, kept, one, 0)
    for way in range(2):
        crossing[way].wait()
        for s in range(3):
            out_ref[s, 0, :, pl.ds(P_KEEP + way * CAP, CAP)] = cross_in[way, s]
    for copy in far:
        copy.wait()


def advance(mesh, fields, cells, offsets, counts):
    n_gx, n_gy = mesh.shape["gx"], mesh.shape["gy"]
    n_fields, levels, width_x, width_y = fields.shape
    columns = n_fields * levels
    packed = (columns * GROUP // LANES * width_x, LANES)
    blocks = cells.shape[2] // LANES
    tile = cells // width_y + 1 + jnp.where(cells % width_y == width_y - 1, levels * width_x, 0)
    f32 = jnp.float32
    vmem = pl.BlockSpec(memory_space=pltpu.VMEM)
    smem = pl.BlockSpec(memory_space=pltpu.SMEM)
    shapes = [(2, columns, LANES), (2, columns, LANES), packed, (8, LANES), offsets.shape]
    return pl.pallas_call(
        functools.partial(advance_kernel, n_gx, n_gy, n_fields, levels, width_x, blocks),
        out_shape=[jax.ShapeDtypeStruct(s, f32) for s in shapes],
        in_specs=[smem, smem, vmem, vmem, pl.BlockSpec(memory_space=pl.ANY)],
        out_specs=[vmem] * 5,
        scratch_shapes=[
            pltpu.VMEM((columns * width_x, LANES), f32),
            pltpu.VMEM((2 * levels * width_x + 1, 8, LANES), f32),
            pltpu.VMEM((4, columns, LANES), f32),
            pltpu.VMEM((3 * levels, LANES), f32),
            pltpu.VMEM(packed, f32),
            pltpu.VMEM(packed, f32),
            pltpu.VMEM(packed, f32),
            pltpu.VMEM((8, LANES), f32),
            pltpu.VMEM((8, LANES), f32),
            pltpu.VMEM((n_gy, 8, LANES), f32),
            pltpu.VMEM((n_gx, 8, LANES), f32),
            pltpu.VMEM((2, 3, 1, CAP), f32),
            pltpu.VMEM((2, 3, 1, CAP), f32),
            pltpu.SemaphoreType.DMA,
            pltpu.SemaphoreType.DMA((9,)),
            pltpu.SemaphoreType.DMA((9,)),
            pltpu.SemaphoreType.DMA((n_gy,)),
            pltpu.SemaphoreType.DMA((n_gy,)),
            pltpu.SemaphoreType.DMA((n_gx,)),
            pltpu.SemaphoreType.DMA((n_gx,)),
        ],
        compiler_params=pltpu.CompilerParams(
            collective_id=0, has_side_effects=True, vmem_limit_bytes=VMEM_BYTES
        ),
    )(tile, counts, cells, offsets, fields.reshape(-1, width_y))


def stencil_kernel(
    levels, width_x, x_ref, vel_ref, prior_ref, heights_ref, low_ref, high_ref, cols_ref, speed_ref,
    new_ref, acc_ref, ext, band,
):
    span = width_x + 16
    step = section_weight * (courant / (speed_ref[0:1, :] + 1e-06))
    zero = jnp.zeros((span, LANES), jnp.float32)
    ext[0:span, :] = zero
    ext[(levels + 1) * span : (levels + 2) * span, :] = zero

    def fill(k, carry):
        start = pl.multiple_of((k + 1) * span + 8, 8)
        ext[pl.ds(start, width_x), :] = x_ref[0, k]
        return carry

    lax.fori_loop(0, levels, fill, 0, unroll=8)
    for d in range(2):
        ext[pl.ds(span + 6 + d, levels, stride=span), :] = low_ref[d]
        ext[pl.ds(span + 8 + width_x + d, levels, stride=span), :] = high_ref[d]
    heights = heights_ref[...]

    @pl.when(pl.program_id(0) == 0)
    def _():
        source = lax.broadcasted_iota(jnp.int32, (2 * LANES, 2 * LANES), 0)
        target = lax.broadcasted_iota(jnp.int32, (2 * LANES, 2 * LANES), 1)
        edge = source - LANES
        outer = jnp.where(edge <= 1, source, jnp.where(edge >= LANES - 2, edge - LANES, 4 * LANES))
        place = jnp.where(source < LANES, source, outer)
        apart = place - jnp.where(target < LANES, target, target - LANES)
        size = jnp.abs(apart)
        slope = jnp.where(size == 1, 8 * apart, jnp.where(size == 2, -apart // 2, 0))
        total = jnp.where(size == 1, 1, 0)
        band[...] = jnp.where(target < LANES, slope, total).astype(jnp.float32).astype(jnp.bfloat16)

    unroll = 4

    def some(n, edges):
        first = n * unroll
        centers = [ext[pl.ds(pl.multiple_of((first + i + 1) * span + 8, 8), width_x), :] for i in range(unroll)]
        sides = [pltpu.roll(edges, unpack_shift(i), 1) for i in range(unroll)]
        both = jnp.concatenate(
            [jnp.concatenate(centers, axis=0), jnp.concatenate(sides, axis=0)], axis=1
        )
        coarse = both.astype(jnp.bfloat16)
        fine = (both - coarse.astype(jnp.float32)).astype(jnp.bfloat16)
        across = jnp.dot(coarse, band[...], preferred_element_type=jnp.float32)
        across += jnp.dot(fine, band[...], preferred_element_type=jnp.float32)
        for i in range(unroll):
            k = first + i
            base = pl.multiple_of((k + 1) * span, 8)
            center = centers[i]
            mine = across[i * width_x : (i + 1) * width_x]

            def along(d):
                return ext[pl.ds(base + 8 + d, width_x), :]

            up = ext[pl.ds(base + span + 8, width_x), :]
            down = ext[pl.ds(base - span + 8, width_x), :]
            low1, high1 = along(-1), along(1)
            grad_x = (high1 - low1) * 8.0 - (along(2) - along(-2))
            turn = vel_ref[0, k] * grad_x + vel_ref[1, k] * mine[:, :LANES]
            laplace = high1 + low1 + mine[:, LANES:] + up + down - 6.0 * center
            tendency = viscosity * laplace - (turn * (1.0 / 12.0) + vel_ref[2, k] * (0.5 * (up - down)))
            acc = prior_weight * prior_ref[0, k] + tendency
            fluid = k >= heights
            acc_ref[0, k] = jnp.where(fluid, acc, 0.0)
            new_ref[0, k] = jnp.where(fluid, center + step * acc, 0.0)
        return pltpu.roll(edges, LANES - GROUP * unroll, 1)

    steps = LANES // GROUP // unroll
    for half in range(levels // (steps * unroll)):
        lax.fori_loop(half * steps, (half + 1) * steps, some, cols_ref[0, half])


def stencil(fields, previous, heights, low, high, cols, speed):
    n_fields, levels, width_x, width_y = fields.shape
    halves = levels * GROUP // LANES
    block = pl.BlockSpec((1, levels, width_x, width_y), lambda f: (f, 0, 0, 0))
    return pl.pallas_call(
        functools.partial(stencil_kernel, levels, width_x),
        grid=(n_fields,),
        out_shape=[jax.ShapeDtypeStruct(fields.shape, jnp.float32)] * 2,
        in_specs=[
            block,
            pl.BlockSpec((3, levels, width_x, width_y), lambda f: (0, 0, 0, 0)),
            block,
            pl.BlockSpec((width_x, width_y), lambda f: (0, 0)),
            pl.BlockSpec((2, levels, LANES), lambda f: (0, f, 0)),
            pl.BlockSpec((2, levels, LANES), lambda f: (0, f, 0)),
            pl.BlockSpec((1, halves, width_x, LANES), lambda f: (f, 0, 0, 0)),
            pl.BlockSpec((8, LANES), lambda f: (0, 0)),
        ],
        out_specs=[block, block],
        scratch_shapes=[
            pltpu.VMEM(((levels + 2) * (width_x + 16), LANES), jnp.float32),
            pltpu.VMEM((2 * LANES, 2 * LANES), jnp.bfloat16),
        ],
        compiler_params=pltpu.CompilerParams(vmem_limit_bytes=VMEM_BYTES),
    )(fields, fields, previous, heights, low, high, cols.reshape(n_fields, halves, width_x, LANES), speed)


def local(mesh, fields, previous, heights, part_cells, part_offsets, cross_counts):
    low, high, cols, speed, moved = advance(
        mesh, fields, part_cells, part_offsets, cross_counts
    )
    updated, accumulated = stencil(fields, previous, heights, low, high, cols, speed)
    return (updated, accumulated, moved)


def solution(mesh):
    placed = (
        P(None, None, "gx", "gy"),
        P(None, None, "gx", "gy"),
        P("gx", "gy"),
        P("gx", "gy", None),
        P(None, "gx", "gy", None),
        P("gx", "gy", None),
    )
    return jax.shard_map(
        functools.partial(local, mesh),
        mesh=mesh,
        in_specs=placed,
        out_specs=(P(None, None, "gx", "gy"), P(None, None, "gx", "gy"), P(None, "gx", "gy", None)),
        check_vma=False,
    )
```

```python
import functools

import jax
import jax.numpy as jnp
from jax import lax
from jax.experimental import pallas as pl
from jax.experimental.pallas import tpu as pltpu
from jax.sharding import PartitionSpec as P

P_KEEP = 8192
CAP = 512
LANES = 128
GROUP = 4
VMEM_BYTES = 60 * 2**20

courant = 0.9
viscosity = 0.1
prior_weight = -5.0 / 9.0
section_weight = 15.0 / 16.0

MESH = pl.DeviceIdType.MESH


def lane_ids(rows):
    return lax.broadcasted_iota(jnp.int32, (rows, LANES), 1)


def unpack_shift(i):
    return LANES - 2 - GROUP * i


def advance_kernel(
    n_gx, n_gy, n_fields, levels, width_x, blocks,
    tile_ref, counts_ref, cell_ref, off_ref, x_hbm,
    low_ref, high_ref, cols_ref, speed_ref, out_ref,
    x_ref, table, planes, corner_ref, packed, from_left, from_right, speed_own, speed_row, speed_y, speed_x,
    cross_own, cross_in,
    load_sem, send_sems, recv_sems, y_send, y_recv, x_send, x_recv,
):
    p = lax.axis_index("gx")
    q = lax.axis_index("gy")

    def at(dp, dq):
        return (lax.rem(p + dp + n_gx, n_gx), lax.rem(q + dq + n_gy, n_gy))

    load = pltpu.make_async_copy(x_hbm, x_ref, load_sem)
    load.start()
    barrier = pltpu.get_barrier_semaphore()
    peers = [at(d, 0) for d in range(1, n_gx)] + [at(0, d) for d in range(1, n_gy)]
    peers += [at(-1, -1), at(1, 1)]
    for peer in peers:
        pl.semaphore_signal(barrier, inc=1, device_id=peer, device_id_type=MESH)

    columns = n_fields * levels
    load.wait()
    for slot, row in enumerate((0, 1, width_x - 2, width_x - 1)):
        planes[slot] = x_ref[pl.ds(row, columns, stride=width_x), :]
    pl.semaphore_wait(barrier, len(peers))

    def remote(src, dst, index, peer):
        return pltpu.make_async_remote_copy(
            src_ref=src, dst_ref=dst, send_sem=send_sems.at[index], recv_sem=recv_sems.at[index],
            device_id=peer, device_id_type=MESH,
        )

    used = 3 * levels
    near = [
        remote(planes.at[0, pl.ds(0, used)], high_ref.at[0, pl.ds(0, used)], 0, at(-1, 0)),
        remote(planes.at[0, pl.ds(0, used)], corner_ref, 1, at(-1, -1)),
    ]
    for copy in near:
        copy.start()

    rows = levels * width_x

    def fastest_rows(i, best):
        start = pl.multiple_of(i * 64, 64)
        total = (
            jnp.abs(x_ref[pl.ds(start, 64), :])
            + jnp.abs(x_ref[pl.ds(rows + start, 64), :])
            + jnp.abs(x_ref[pl.ds(2 * rows + start, 64), :])
        )
        return jnp.maximum(best, jnp.max(total.reshape(8, 8, LANES), axis=0))

    speed_own[...] = lax.fori_loop(0, rows // 64, fastest_rows, jnp.zeros((8, LANES), jnp.float32))

    y_copies = []
    for d in range(1, n_gy):
        y_copies.append(
            pltpu.make_async_remote_copy(
                src_ref=speed_own, dst_ref=speed_y.at[d], send_sem=y_send.at[d], recv_sem=y_recv.at[d],
                device_id=at(0, d), device_id_type=MESH,
            )
        )
        y_copies[-1].start()

    lanes = lane_ids(width_x)
    per_pack = LANES // GROUP
    packs = columns // per_pack

    def pack(j, carry):
        total = jnp.zeros((width_x, LANES), jnp.float32)
        for i in range(per_pack):
            start = pl.multiple_of((j * per_pack + i) * width_x, width_x)
            turned = pltpu.roll(x_ref[pl.ds(start, width_x), :], (2 + GROUP * i) % LANES, 1)
            total = jnp.where(lanes // GROUP == i, turned, total)
        packed[pl.ds(pl.multiple_of(j * width_x, width_x), width_x), :] = total
        return carry

    lax.fori_loop(0, packs, pack, 0)
    side = [
        remote(packed, from_right, 2, at(0, -1)),
        remote(packed, from_left, 3, at(0, 1)),
    ]
    for copy in side:
        copy.start()
    rest = columns - used
    far = [
        remote(planes.at[0, pl.ds(used, rest)], high_ref.at[0, pl.ds(used, rest)], 4, at(-1, 0)),
        remote(planes.at[1], high_ref.at[1], 5, at(-1, 0)),
        remote(planes.at[pl.ds(2, 2)], low_ref, 6, at(1, 0)),
    ]

    best = speed_own[...]
    for d in range(1, n_gy):
        y_copies[d - 1].wait()
        best = jnp.maximum(best, speed_y[d])
    speed_row[...] = best
    x_copies = []
    for d in range(1, n_gx):
        x_copies.append(
            pltpu.make_async_remote_copy(
                src_ref=speed_row, dst_ref=speed_x.at[d], send_sem=x_send.at[d], recv_sem=x_recv.at[d],
                device_id=at(d, 0), device_id_type=MESH,
            )
        )
        x_copies[-1].start()
    for copy in far:
        copy.start()

    def build_own(k, carry):
        base = k * width_x + 1
        for s in range(3):
            own = x_ref[pl.ds(pl.multiple_of(s * rows + k * width_x, 8), width_x), :]
            table[pl.ds(base, width_x), s, :] = own
            table[pl.ds(base - 1, width_x), 3 + s, :] = own
        return carry

    lax.fori_loop(0, levels, build_own, 0, unroll=2)

    for copy in side:
        copy.wait()
    has_left = jnp.where(q > 0, 1.0, 0.0)
    has_right = jnp.where(q < n_gy - 1, 1.0, 0.0)
    for j in range(packs):
        here = pl.ds(j * width_x, width_x)
        cols_ref[here, :] = jnp.where(
            lanes % GROUP < 2, from_left[here, :] * has_left, from_right[here, :] * has_right
        )

    def build_turned(j, carry):
        for i in range(per_pack):
            k = j * per_pack + i
            base = k * width_x + 1 + rows
            for s in range(3):
                own = x_ref[pl.ds(pl.multiple_of(s * rows + k * width_x, 8), width_x), :]
                start = pl.multiple_of((s * (levels // per_pack) + j) * width_x, 8)
                edge = pltpu.roll(cols_ref[pl.ds(start, width_x), :], unpack_shift(i), 1)
                turned = jnp.where(lanes == 0, edge, own)
                table[pl.ds(base, width_x), s, :] = turned
                table[pl.ds(base - 1, width_x), 3 + s, :] = turned
        return carry

    lax.fori_loop(0, levels // per_pack, build_turned, 0)
    for copy in near:
        copy.wait()
    first = lane_ids(levels) == 0
    for s in range(3):
        plane = high_ref[0, s * levels : (s + 1) * levels, :]
        corner = corner_ref[s * levels : (s + 1) * levels, :] * has_right
        table[pl.ds(width_x, levels, stride=width_x), 3 + s, :] = plane
        table[pl.ds(rows + width_x, levels, stride=width_x), 3 + s, :] = jnp.where(
            first, corner, plane
        )

    for d in range(1, n_gx):
        x_copies[d - 1].wait()
        best = jnp.maximum(best, speed_x[d])
    fastest = jnp.broadcast_to(jnp.max(best, keepdims=True), (8, LANES))
    speed_ref[...] = fastest
    time_step = courant / (fastest[0:1, :] + 1e-06)

    half = LANES // 2
    lanes = lane_ids(8)
    sub = lax.broadcasted_iota(jnp.int32, (8, LANES), 0)
    place = lanes % half

    def one(j, carry):
        sums = []
        here = pl.ds(pl.multiple_of(j * LANES, LANES), LANES)
        column = cell_ref[0, :, here] % LANES
        column_other = pltpu.roll(column, half, 1)
        frac = off_ref[1, 0, :, here]
        other = pltpu.roll(frac, half, 1)
        early = lanes[0:1] < half
        for h in range(2):
            if h == 0:
                ids = jnp.where(early, column, (column_other + 1) % LANES)
                weight = jnp.where(early, 1.0 - frac, other)
            else:
                ids = jnp.where(early, column_other, (column + 1) % LANES)
                weight = jnp.where(early, 1.0 - other, frac)
            ids = jnp.broadcast_to(ids, (8, LANES))
            got = jnp.zeros((8, LANES), jnp.float32)
            for i in range(half):
                tile = table[tile_ref[j, h * half + i]]
                turned = jnp.take_along_axis(tile, ids, axis=1, mode="promise_in_bounds")
                got = jnp.where(place == i, turned, got)
            got = got * weight
            sums.append(got + pltpu.roll(got, half, 1))
        both = jnp.where(lanes < half, sums[0], sums[1])
        frac = off_ref[0, 0, :, here]
        both = both * jnp.where(sub < 3, 1.0 - frac, frac)
        vel = both[0:3] + both[3:6]
        for s in range(3):
            out_ref[s, 0, :, here] = off_ref[s, 0, :, here] + time_step * vel[s : s + 1]
        return carry

    kept = P_KEEP // LANES
    lax.fori_loop(kept, blocks, one, 0)
    slots = lax.broadcasted_iota(jnp.int32, (1, CAP), 1)
    crossing = []
    for way in range(2):
        live = jnp.where(slots < counts_ref[0, 0, way], 1.0, 0.0)
        for s in range(3):
            cross_own[way, s] = out_ref[s, 0, :, pl.ds(P_KEEP + way * CAP, CAP)] * live
        crossing.append(remote(cross_own.at[way], cross_in.at[way], 7 + way, at(1 - 2 * way, 0)))
        crossing[-1].start()
    lax.fori_loop(0, kept, one, 0)
    for way in range(2):
        crossing[way].wait()
        for s in range(3):
            out_ref[s, 0, :, pl.ds(P_KEEP + way * CAP, CAP)] = cross_in[way, s]
    for copy in far:
        copy.wait()


def advance(mesh, fields, cells, offsets, counts):
    n_gx, n_gy = mesh.shape["gx"], mesh.shape["gy"]
    n_fields, levels, width_x, width_y = fields.shape
    columns = n_fields * levels
    packed = (columns * GROUP // LANES * width_x, LANES)
    blocks = cells.shape[2] // LANES
    tile = cells // width_y + 1 + jnp.where(cells % width_y == width_y - 1, levels * width_x, 0)
    f32 = jnp.float32
    vmem = pl.BlockSpec(memory_space=pltpu.VMEM)
    smem = pl.BlockSpec(memory_space=pltpu.SMEM)
    shapes = [(2, columns, LANES), (2, columns, LANES), packed, (8, LANES), offsets.shape]
    return pl.pallas_call(
        functools.partial(advance_kernel, n_gx, n_gy, n_fields, levels, width_x, blocks),
        out_shape=[jax.ShapeDtypeStruct(s, f32) for s in shapes],
        in_specs=[smem, smem, vmem, vmem, pl.BlockSpec(memory_space=pl.ANY)],
        out_specs=[vmem] * 5,
        scratch_shapes=[
            pltpu.VMEM((columns * width_x, LANES), f32),
            pltpu.VMEM((2 * levels * width_x + 1, 8, LANES), f32),
            pltpu.VMEM((4, columns, LANES), f32),
            pltpu.VMEM((3 * levels, LANES), f32),
            pltpu.VMEM(packed, f32),
            pltpu.VMEM(packed, f32),
            pltpu.VMEM(packed, f32),
            pltpu.VMEM((8, LANES), f32),
            pltpu.VMEM((8, LANES), f32),
            pltpu.VMEM((n_gy, 8, LANES), f32),
            pltpu.VMEM((n_gx, 8, LANES), f32),
            pltpu.VMEM((2, 3, 1, CAP), f32),
            pltpu.VMEM((2, 3, 1, CAP), f32),
            pltpu.SemaphoreType.DMA,
            pltpu.SemaphoreType.DMA((9,)),
            pltpu.SemaphoreType.DMA((9,)),
            pltpu.SemaphoreType.DMA((n_gy,)),
            pltpu.SemaphoreType.DMA((n_gy,)),
            pltpu.SemaphoreType.DMA((n_gx,)),
            pltpu.SemaphoreType.DMA((n_gx,)),
        ],
        compiler_params=pltpu.CompilerParams(
            collective_id=0, has_side_effects=True, vmem_limit_bytes=VMEM_BYTES
        ),
    )(tile.reshape(blocks, LANES), counts, cells, offsets, fields.reshape(-1, width_y))


def stencil_kernel(
    levels, width_x, x_ref, vel_ref, prior_ref, heights_ref, low_ref, high_ref, cols_ref, speed_ref,
    new_ref, acc_ref, ext, band, halves, across,
):
    span = width_x + 16
    step = section_weight * (courant / (speed_ref[0:1, :] + 1e-06))
    zero = jnp.zeros((span, LANES), jnp.float32)
    ext[0:span, :] = zero
    ext[(levels + 1) * span : (levels + 2) * span, :] = zero

    def fill(k, carry):
        start = pl.multiple_of((k + 1) * span + 8, 8)
        ext[pl.ds(start, width_x), :] = x_ref[0, k]
        return carry

    lax.fori_loop(0, levels, fill, 0, unroll=8)
    for d in range(2):
        ext[pl.ds(span + 6 + d, levels, stride=span), :] = low_ref[d]
        ext[pl.ds(span + 8 + width_x + d, levels, stride=span), :] = high_ref[d]
    heights = heights_ref[...]

    @pl.when(pl.program_id(0) == 0)
    def _():
        source = lax.broadcasted_iota(jnp.int32, (2 * LANES, 2 * LANES), 0)
        target = lax.broadcasted_iota(jnp.int32, (2 * LANES, 2 * LANES), 1)
        edge = source - LANES
        outer = jnp.where(edge <= 1, source, jnp.where(edge >= LANES - 2, edge - LANES, 4 * LANES))
        place = jnp.where(source < LANES, source, outer)
        apart = place - jnp.where(target < LANES, target, target - LANES)
        size = jnp.abs(apart)
        slope = jnp.where(size == 1, 8 * apart, jnp.where(size == 2, -apart // 2, 0))
        total = jnp.where(size == 1, 1, 0)
        band[...] = jnp.where(target < LANES, slope, total).astype(jnp.float32).astype(jnp.bfloat16)

    unroll = 4
    rows = levels * width_x

    def split(n, edges):
        for i in range(unroll):
            k = n * unroll + i
            side = pltpu.roll(edges, unpack_shift(i), 1)
            for part, value in enumerate((x_ref[0, k], side)):
                coarse = value.astype(jnp.bfloat16)
                fine = (value - coarse.astype(jnp.float32)).astype(jnp.bfloat16)
                here = pl.ds(part * LANES, LANES)
                halves[pl.ds(pl.multiple_of(k * width_x, width_x), width_x), here] = coarse
                halves[pl.ds(pl.multiple_of(rows + k * width_x, width_x), width_x), here] = fine
        return pltpu.roll(edges, LANES - GROUP * unroll, 1)

    steps = LANES // GROUP // unroll
    for half in range(levels // (steps * unroll)):
        lax.fori_loop(half * steps, (half + 1) * steps, split, cols_ref[0, half])
    across[...] = jnp.dot(halves[0:rows], band[...], preferred_element_type=jnp.float32) + jnp.dot(
        halves[rows:], band[...], preferred_element_type=jnp.float32
    )

    def some(n, carry):
        first = n * unroll
        for i in range(unroll):
            mine = pl.ds(pl.multiple_of((first + i) * width_x, width_x), width_x)
            slope = across[mine, 0:LANES]
            beside = across[mine, LANES : 2 * LANES]
            k = first + i
            base = pl.multiple_of((k + 1) * span, 8)

            def along(d):
                return ext[pl.ds(base + 8 + d, width_x), :]

            center = along(0)
            up = ext[pl.ds(base + span + 8, width_x), :]
            down = ext[pl.ds(base - span + 8, width_x), :]
            low1, high1 = along(-1), along(1)
            grad_x = (high1 - low1) * 8.0 - (along(2) - along(-2))
            turn = vel_ref[0, k] * grad_x + vel_ref[1, k] * slope
            laplace = high1 + low1 + beside + up + down - 6.0 * center
            tendency = viscosity * laplace - (turn * (1.0 / 12.0) + vel_ref[2, k] * (0.5 * (up - down)))
            acc = prior_weight * prior_ref[0, k] + tendency
            fluid = k >= heights
            acc_ref[0, k] = jnp.where(fluid, acc, 0.0)
            new_ref[0, k] = jnp.where(fluid, center + step * acc, 0.0)
        return carry

    lax.fori_loop(0, levels // unroll, some, 0)


def stencil(fields, previous, heights, low, high, cols, speed):
    n_fields, levels, width_x, width_y = fields.shape
    halves = levels * GROUP // LANES
    block = pl.BlockSpec((1, levels, width_x, width_y), lambda f: (f, 0, 0, 0))
    return pl.pallas_call(
        functools.partial(stencil_kernel, levels, width_x),
        grid=(n_fields,),
        out_shape=[jax.ShapeDtypeStruct(fields.shape, jnp.float32)] * 2,
        in_specs=[
            block,
            pl.BlockSpec((3, levels, width_x, width_y), lambda f: (0, 0, 0, 0)),
            block,
            pl.BlockSpec((width_x, width_y), lambda f: (0, 0)),
            pl.BlockSpec((2, levels, LANES), lambda f: (0, f, 0)),
            pl.BlockSpec((2, levels, LANES), lambda f: (0, f, 0)),
            pl.BlockSpec((1, halves, width_x, LANES), lambda f: (f, 0, 0, 0)),
            pl.BlockSpec((8, LANES), lambda f: (0, 0)),
        ],
        out_specs=[block, block],
        scratch_shapes=[
            pltpu.VMEM(((levels + 2) * (width_x + 16), LANES), jnp.float32),
            pltpu.VMEM((2 * LANES, 2 * LANES), jnp.bfloat16),
            pltpu.VMEM((2 * levels * width_x, 2 * LANES), jnp.bfloat16),
            pltpu.VMEM((levels * width_x, 2 * LANES), jnp.float32),
        ],
        compiler_params=pltpu.CompilerParams(vmem_limit_bytes=VMEM_BYTES),
    )(fields, fields, previous, heights, low, high, cols.reshape(n_fields, halves, width_x, LANES), speed)


def local(mesh, fields, previous, heights, part_cells, part_offsets, cross_counts):
    low, high, cols, speed, moved = advance(
        mesh, fields, part_cells, part_offsets, cross_counts
    )
    updated, accumulated = stencil(fields, previous, heights, low, high, cols, speed)
    return (updated, accumulated, moved)


def solution(mesh):
    placed = (
        P(None, None, "gx", "gy"),
        P(None, None, "gx", "gy"),
        P("gx", "gy"),
        P("gx", "gy", None),
        P(None, "gx", "gy", None),
        P("gx", "gy", None),
    )
    return jax.shard_map(
        functools.partial(local, mesh),
        mesh=mesh,
        in_specs=placed,
        out_specs=(P(None, None, "gx", "gy"), P(None, None, "gx", "gy"), P(None, "gx", "gy", None)),
        check_vma=False,
    )
```

```python
import functools
import math

import jax
import jax.numpy as jnp
from jax import lax
from jax.experimental import pallas as pl
from jax.experimental.pallas import tpu as pltpu
from jax.sharding import PartitionSpec as P

P_KEEP = 8192
CAP = 512
LANES = 128
GROUP = 4
VMEM_BYTES = 60 * 2**20

courant = 0.9
viscosity = 0.1
prior_weight = -5.0 / 9.0
section_weight = 15.0 / 16.0

MESH = pl.DeviceIdType.MESH


def lane_ids(rows):
    return lax.broadcasted_iota(jnp.int32, (rows, LANES), 1)


def unpack_shift(i):
    return LANES - 2 - GROUP * i


def advance_kernel(
    n_gx, n_gy, n_fields, levels, width_x, blocks,
    tile_ref, counts_ref, cell_ref, off_ref, x_hbm,
    low_ref, high_ref, cols_ref, speed_ref, out_ref,
    x_ref, table, planes, corner_ref, packed, from_left, from_right, speed_own, speed_row, speed_y, speed_x,
    cross_own, cross_in, ids_rows, got_rows,
    load_sem, send_sems, recv_sems, y_send, y_recv, x_send, x_recv,
):
    p = lax.axis_index("gx")
    q = lax.axis_index("gy")

    def at(dp, dq):
        return (lax.rem(p + dp + n_gx, n_gx), lax.rem(q + dq + n_gy, n_gy))

    load = pltpu.make_async_copy(x_hbm, x_ref, load_sem)
    load.start()
    barrier = pltpu.get_barrier_semaphore()
    peers = [at(d, 0) for d in range(1, n_gx)] + [at(0, d) for d in range(1, n_gy)]
    peers += [at(-1, -1), at(1, 1)]
    for peer in peers:
        pl.semaphore_signal(barrier, inc=1, device_id=peer, device_id_type=MESH)

    columns = n_fields * levels
    load.wait()
    for slot, row in enumerate((0, 1, width_x - 2, width_x - 1)):
        planes[slot] = x_ref[pl.ds(row, columns, stride=width_x), :]
    pl.semaphore_wait(barrier, len(peers))

    def remote(src, dst, index, peer):
        return pltpu.make_async_remote_copy(
            src_ref=src, dst_ref=dst, send_sem=send_sems.at[index], recv_sem=recv_sems.at[index],
            device_id=peer, device_id_type=MESH,
        )

    used = 3 * levels
    near = [
        remote(planes.at[0, pl.ds(0, used)], high_ref.at[0, pl.ds(0, used)], 0, at(-1, 0)),
        remote(planes.at[0, pl.ds(0, used)], corner_ref, 1, at(-1, -1)),
    ]
    for copy in near:
        copy.start()

    rows = levels * width_x

    def fastest_rows(i, best):
        start = pl.multiple_of(i * 64, 64)
        total = (
            jnp.abs(x_ref[pl.ds(start, 64), :])
            + jnp.abs(x_ref[pl.ds(rows + start, 64), :])
            + jnp.abs(x_ref[pl.ds(2 * rows + start, 64), :])
        )
        return jnp.maximum(best, jnp.max(total.reshape(8, 8, LANES), axis=0))

    speed_own[...] = lax.fori_loop(0, rows // 64, fastest_rows, jnp.zeros((8, LANES), jnp.float32))

    y_copies = []
    for d in range(1, n_gy):
        y_copies.append(
            pltpu.make_async_remote_copy(
                src_ref=speed_own, dst_ref=speed_y.at[d], send_sem=y_send.at[d], recv_sem=y_recv.at[d],
                device_id=at(0, d), device_id_type=MESH,
            )
        )
        y_copies[-1].start()

    lanes = lane_ids(width_x)
    per_pack = LANES // GROUP
    packs = columns // per_pack

    def pack(j, carry):
        total = jnp.zeros((width_x, LANES), jnp.float32)
        for i in range(per_pack):
            start = pl.multiple_of((j * per_pack + i) * width_x, width_x)
            turned = pltpu.roll(x_ref[pl.ds(start, width_x), :], (2 + GROUP * i) % LANES, 1)
            total = jnp.where(lanes // GROUP == i, turned, total)
        packed[pl.ds(pl.multiple_of(j * width_x, width_x), width_x), :] = total
        return carry

    lax.fori_loop(0, packs, pack, 0)
    side = [
        remote(packed, from_right, 2, at(0, -1)),
        remote(packed, from_left, 3, at(0, 1)),
    ]
    for copy in side:
        copy.start()
    rest = columns - used
    far = [
        remote(planes.at[0, pl.ds(used, rest)], high_ref.at[0, pl.ds(used, rest)], 4, at(-1, 0)),
        remote(planes.at[1], high_ref.at[1], 5, at(-1, 0)),
        remote(planes.at[pl.ds(2, 2)], low_ref, 6, at(1, 0)),
    ]

    best = speed_own[...]
    for d in range(1, n_gy):
        y_copies[d - 1].wait()
        best = jnp.maximum(best, speed_y[d])
    speed_row[...] = best
    x_copies = []
    for d in range(1, n_gx):
        x_copies.append(
            pltpu.make_async_remote_copy(
                src_ref=speed_row, dst_ref=speed_x.at[d], send_sem=x_send.at[d], recv_sem=x_recv.at[d],
                device_id=at(d, 0), device_id_type=MESH,
            )
        )
        x_copies[-1].start()
    for copy in far:
        copy.start()

    def build_own(k, carry):
        base = k * width_x + 1
        for s in range(3):
            own = x_ref[pl.ds(pl.multiple_of(s * rows + k * width_x, 8), width_x), :]
            table[pl.ds(base, width_x), s, :] = own
            table[pl.ds(base - 1, width_x), 3 + s, :] = own
        return carry

    lax.fori_loop(0, levels, build_own, 0, unroll=2)
    turn = LANES // 2
    early_lane = lane_ids(1) < turn

    def columns_of(j, carry):
        column = cell_ref[0, :, pl.ds(pl.multiple_of(j * LANES, LANES), LANES)] % LANES
        other = pltpu.roll(column, turn, 1)
        ids_rows[pl.ds(2 * j, 1), :] = jnp.where(early_lane, column, (other + 1) % LANES)
        ids_rows[pl.ds(2 * j + 1, 1), :] = jnp.where(early_lane, other, (column + 1) % LANES)
        return carry

    lax.fori_loop(0, blocks, columns_of, 0, unroll=4)

    for copy in side:
        copy.wait()
    has_left = jnp.where(q > 0, 1.0, 0.0)
    has_right = jnp.where(q < n_gy - 1, 1.0, 0.0)
    for j in range(packs):
        here = pl.ds(j * width_x, width_x)
        cols_ref[here, :] = jnp.where(
            lanes % GROUP < 2, from_left[here, :] * has_left, from_right[here, :] * has_right
        )

    def build_turned(j, carry):
        for i in range(per_pack):
            k = j * per_pack + i
            base = k * width_x + 1 + rows
            for s in range(3):
                own = x_ref[pl.ds(pl.multiple_of(s * rows + k * width_x, 8), width_x), :]
                start = pl.multiple_of((s * (levels // per_pack) + j) * width_x, 8)
                edge = pltpu.roll(cols_ref[pl.ds(start, width_x), :], unpack_shift(i), 1)
                turned = jnp.where(lanes == 0, edge, own)
                table[pl.ds(base, width_x), s, :] = turned
                table[pl.ds(base - 1, width_x), 3 + s, :] = turned
        return carry

    lax.fori_loop(0, levels // per_pack, build_turned, 0)
    for copy in near:
        copy.wait()
    first = lane_ids(levels) == 0
    for s in range(3):
        plane = high_ref[0, s * levels : (s + 1) * levels, :]
        corner = corner_ref[s * levels : (s + 1) * levels, :] * has_right
        table[pl.ds(width_x, levels, stride=width_x), 3 + s, :] = plane
        table[pl.ds(rows + width_x, levels, stride=width_x), 3 + s, :] = jnp.where(
            first, corner, plane
        )

    for d in range(1, n_gx):
        x_copies[d - 1].wait()
        best = jnp.maximum(best, speed_x[d])
    fastest = jnp.broadcast_to(jnp.max(best, keepdims=True), (8, LANES))
    speed_ref[...] = fastest
    time_step = courant / (fastest[0:1, :] + 1e-06)

    half = LANES // 2
    lanes = lane_ids(8)
    sub = lax.broadcasted_iota(jnp.int32, (8, LANES), 0)
    place = lanes % half

    def gather(j, carry):
        for h in range(2):
            ids = jnp.broadcast_to(ids_rows[pl.ds(2 * j + h, 1), :], (8, LANES))
            got = jnp.zeros((8, LANES), jnp.float32)
            for i in range(half):
                tile = table[tile_ref[j, h * half + i]]
                turned = jnp.take_along_axis(tile, ids, axis=1, mode="promise_in_bounds")
                got = jnp.where(place == i, turned, got)
            got_rows[2 * j + h] = got
        return carry

    def finish(j):
        here = pl.ds(pl.multiple_of(j * LANES, LANES), LANES)
        frac = off_ref[1, 0, :, here]
        other = pltpu.roll(frac, half, 1)
        early = lanes[0:1] < half
        first = got_rows[2 * j] * jnp.where(early, 1.0 - frac, other)
        second = got_rows[2 * j + 1] * jnp.where(early, 1.0 - other, frac)
        both = jnp.where(lanes < half, first + pltpu.roll(first, half, 1), second + pltpu.roll(second, half, 1))
        frac = off_ref[0, 0, :, here]
        both = both * jnp.where(sub < 3, 1.0 - frac, frac)
        vel = both[0:3] + both[3:6]
        for s in range(3):
            out_ref[s, 0, :, here] = off_ref[s, 0, :, here] + time_step * vel[s : s + 1]

    group = math.gcd(math.gcd(P_KEEP // LANES, 2 * CAP // LANES), 4)

    def finish_some(n, carry):
        for i in range(group):
            finish(n * group + i)
        return carry

    kept = P_KEEP // LANES
    lax.fori_loop(kept, blocks, gather, 0)
    lax.fori_loop(kept // group, blocks // group, finish_some, 0)
    slots = lax.broadcasted_iota(jnp.int32, (1, CAP), 1)
    crossing = []
    for way in range(2):
        live = jnp.where(slots < counts_ref[0, 0, way], 1.0, 0.0)
        for s in range(3):
            cross_own[way, s] = out_ref[s, 0, :, pl.ds(P_KEEP + way * CAP, CAP)] * live
        crossing.append(remote(cross_own.at[way], cross_in.at[way], 7 + way, at(1 - 2 * way, 0)))
        crossing[-1].start()
    lax.fori_loop(0, kept, gather, 0)
    lax.fori_loop(0, kept // group, finish_some, 0)
    for way in range(2):
        crossing[way].wait()
        for s in range(3):
            out_ref[s, 0, :, pl.ds(P_KEEP + way * CAP, CAP)] = cross_in[way, s]
    for copy in far:
        copy.wait()


def advance(mesh, fields, cells, offsets, counts):
    n_gx, n_gy = mesh.shape["gx"], mesh.shape["gy"]
    n_fields, levels, width_x, width_y = fields.shape
    columns = n_fields * levels
    packed = (columns * GROUP // LANES * width_x, LANES)
    blocks = cells.shape[2] // LANES
    tile = cells // width_y + 1 + jnp.where(cells % width_y == width_y - 1, levels * width_x, 0)
    f32 = jnp.float32
    vmem = pl.BlockSpec(memory_space=pltpu.VMEM)
    smem = pl.BlockSpec(memory_space=pltpu.SMEM)
    shapes = [(2, columns, LANES), (2, columns, LANES), packed, (8, LANES), offsets.shape]
    return pl.pallas_call(
        functools.partial(advance_kernel, n_gx, n_gy, n_fields, levels, width_x, blocks),
        out_shape=[jax.ShapeDtypeStruct(s, f32) for s in shapes],
        in_specs=[smem, smem, vmem, vmem, pl.BlockSpec(memory_space=pl.ANY)],
        out_specs=[vmem] * 5,
        scratch_shapes=[
            pltpu.VMEM((columns * width_x, LANES), f32),
            pltpu.VMEM((2 * levels * width_x + 1, 8, LANES), f32),
            pltpu.VMEM((4, columns, LANES), f32),
            pltpu.VMEM((3 * levels, LANES), f32),
            pltpu.VMEM(packed, f32),
            pltpu.VMEM(packed, f32),
            pltpu.VMEM(packed, f32),
            pltpu.VMEM((8, LANES), f32),
            pltpu.VMEM((8, LANES), f32),
            pltpu.VMEM((n_gy, 8, LANES), f32),
            pltpu.VMEM((n_gx, 8, LANES), f32),
            pltpu.VMEM((2, 3, 1, CAP), f32),
            pltpu.VMEM((2, 3, 1, CAP), f32),
            pltpu.VMEM((2 * blocks, LANES), jnp.int32),
            pltpu.VMEM((2 * blocks, 8, LANES), f32),
            pltpu.SemaphoreType.DMA,
            pltpu.SemaphoreType.DMA((9,)),
            pltpu.SemaphoreType.DMA((9,)),
            pltpu.SemaphoreType.DMA((n_gy,)),
            pltpu.SemaphoreType.DMA((n_gy,)),
            pltpu.SemaphoreType.DMA((n_gx,)),
            pltpu.SemaphoreType.DMA((n_gx,)),
        ],
        compiler_params=pltpu.CompilerParams(
            collective_id=0, has_side_effects=True, vmem_limit_bytes=VMEM_BYTES
        ),
    )(tile.reshape(blocks, LANES), counts, cells, offsets, fields.reshape(-1, width_y))


def stencil_kernel(
    levels, width_x, x_ref, vel_ref, prior_ref, heights_ref, low_ref, high_ref, cols_ref, speed_ref,
    new_ref, acc_ref, ext, band, halves, across,
):
    span = width_x + 16
    step = section_weight * (courant / (speed_ref[0:1, :] + 1e-06))
    zero = jnp.zeros((span, LANES), jnp.float32)
    ext[0:span, :] = zero
    ext[(levels + 1) * span : (levels + 2) * span, :] = zero

    def fill(k, carry):
        start = pl.multiple_of((k + 1) * span + 8, 8)
        ext[pl.ds(start, width_x), :] = x_ref[0, k]
        return carry

    lax.fori_loop(0, levels, fill, 0, unroll=8)
    for d in range(2):
        ext[pl.ds(span + 6 + d, levels, stride=span), :] = low_ref[d]
        ext[pl.ds(span + 8 + width_x + d, levels, stride=span), :] = high_ref[d]
    heights = heights_ref[...]

    @pl.when(pl.program_id(0) == 0)
    def _():
        source = lax.broadcasted_iota(jnp.int32, (2 * LANES, 2 * LANES), 0)
        target = lax.broadcasted_iota(jnp.int32, (2 * LANES, 2 * LANES), 1)
        edge = source - LANES
        outer = jnp.where(edge <= 1, source, jnp.where(edge >= LANES - 2, edge - LANES, 4 * LANES))
        place = jnp.where(source < LANES, source, outer)
        apart = place - jnp.where(target < LANES, target, target - LANES)
        size = jnp.abs(apart)
        slope = jnp.where(size == 1, 8 * apart, jnp.where(size == 2, -apart // 2, 0))
        total = jnp.where(size == 1, 1, 0)
        band[...] = jnp.where(target < LANES, slope, total).astype(jnp.float32).astype(jnp.bfloat16)

    unroll = 4
    rows = levels * width_x

    def split(n, edges):
        for i in range(unroll):
            k = n * unroll + i
            side = pltpu.roll(edges, unpack_shift(i), 1)
            for part, value in enumerate((x_ref[0, k], side)):
                coarse = value.astype(jnp.bfloat16)
                fine = (value - coarse.astype(jnp.float32)).astype(jnp.bfloat16)
                here = pl.ds(part * LANES, LANES)
                halves[pl.ds(pl.multiple_of(k * width_x, width_x), width_x), here] = coarse
                halves[pl.ds(pl.multiple_of(rows + k * width_x, width_x), width_x), here] = fine
        return pltpu.roll(edges, LANES - GROUP * unroll, 1)

    steps = LANES // GROUP // unroll
    for half in range(levels // (steps * unroll)):
        lax.fori_loop(half * steps, (half + 1) * steps, split, cols_ref[0, half])
    across[...] = jnp.dot(halves[0:rows], band[...], preferred_element_type=jnp.float32) + jnp.dot(
        halves[rows:], band[...], preferred_element_type=jnp.float32
    )

    def some(n, carry):
        first = n * unroll
        for i in range(unroll):
            mine = pl.ds(pl.multiple_of((first + i) * width_x, width_x), width_x)
            slope = across[mine, 0:LANES]
            beside = across[mine, LANES : 2 * LANES]
            k = first + i
            base = pl.multiple_of((k + 1) * span, 8)

            def along(d):
                return ext[pl.ds(base + 8 + d, width_x), :]

            center = along(0)
            up = ext[pl.ds(base + span + 8, width_x), :]
            down = ext[pl.ds(base - span + 8, width_x), :]
            low1, high1 = along(-1), along(1)
            grad_x = (high1 - low1) * 8.0 - (along(2) - along(-2))
            turn = vel_ref[0, k] * grad_x + vel_ref[1, k] * slope
            laplace = high1 + low1 + beside + up + down - 6.0 * center
            tendency = viscosity * laplace - (turn * (1.0 / 12.0) + vel_ref[2, k] * (0.5 * (up - down)))
            acc = prior_weight * prior_ref[0, k] + tendency
            fluid = k >= heights
            acc_ref[0, k] = jnp.where(fluid, acc, 0.0)
            new_ref[0, k] = jnp.where(fluid, center + step * acc, 0.0)
        return carry

    lax.fori_loop(0, levels // unroll, some, 0)


def stencil(fields, previous, heights, low, high, cols, speed):
    n_fields, levels, width_x, width_y = fields.shape
    halves = levels * GROUP // LANES
    block = pl.BlockSpec((1, levels, width_x, width_y), lambda f: (f, 0, 0, 0))
    return pl.pallas_call(
        functools.partial(stencil_kernel, levels, width_x),
        grid=(n_fields,),
        out_shape=[jax.ShapeDtypeStruct(fields.shape, jnp.float32)] * 2,
        in_specs=[
            block,
            pl.BlockSpec((3, levels, width_x, width_y), lambda f: (0, 0, 0, 0)),
            block,
            pl.BlockSpec((width_x, width_y), lambda f: (0, 0)),
            pl.BlockSpec((2, levels, LANES), lambda f: (0, f, 0)),
            pl.BlockSpec((2, levels, LANES), lambda f: (0, f, 0)),
            pl.BlockSpec((1, halves, width_x, LANES), lambda f: (f, 0, 0, 0)),
            pl.BlockSpec((8, LANES), lambda f: (0, 0)),
        ],
        out_specs=[block, block],
        scratch_shapes=[
            pltpu.VMEM(((levels + 2) * (width_x + 16), LANES), jnp.float32),
            pltpu.VMEM((2 * LANES, 2 * LANES), jnp.bfloat16),
            pltpu.VMEM((2 * levels * width_x, 2 * LANES), jnp.bfloat16),
            pltpu.VMEM((levels * width_x, 2 * LANES), jnp.float32),
        ],
        compiler_params=pltpu.CompilerParams(vmem_limit_bytes=VMEM_BYTES),
    )(fields, fields, previous, heights, low, high, cols.reshape(n_fields, halves, width_x, LANES), speed)


def local(mesh, fields, previous, heights, part_cells, part_offsets, cross_counts):
    low, high, cols, speed, moved = advance(
        mesh, fields, part_cells, part_offsets, cross_counts
    )
    updated, accumulated = stencil(fields, previous, heights, low, high, cols, speed)
    return (updated, accumulated, moved)


def solution(mesh):
    placed = (
        P(None, None, "gx", "gy"),
        P(None, None, "gx", "gy"),
        P("gx", "gy"),
        P("gx", "gy", None),
        P(None, "gx", "gy", None),
        P("gx", "gy", None),
    )
    return jax.shard_map(
        functools.partial(local, mesh),
        mesh=mesh,
        in_specs=placed,
        out_specs=(P(None, None, "gx", "gy"), P(None, None, "gx", "gy"), P(None, "gx", "gy", None)),
        check_vma=False,
    )
```
